256 devices in a mesh: batch: 4 (over y), patch: 16 (over z_hi, x, core), tensor: 4 (over z_lo).
Axes of the slice: x: 4, y: 4, z: 8 (z_hi: 2, z_lo: 4; z = z_hi * 4 + z_lo), core: 2. Of those that a mesh axis runs over, the one named last changes fastest.
Arguments:
- image: bfloat16 [32768, 3072], P(('batch', 'patch'), 'tensor'), parts along dimension 0, may hold values from -6 to 6
- modulation: float32 [12, 3072], P('batch'), parts along dimension 0, may hold values from -4 to 4
- w_query: bfloat16 [3072, 1536], P(None, 'tensor'), may hold values from -0.109375 to 0.109375
- w_key: bfloat16 [3072, 1536], P(None, 'tensor'), may hold values from -0.109375 to 0.109375
- w_value: bfloat16 [3072, 1536], P(None, 'tensor'), may hold values from -0.109375 to 0.109375
- w_out: bfloat16 [1536, 3072], P('tensor'), may hold values from -0.15625 to 0.15625
- query_gain: float32 [128], replicated, may hold values from 1.2 to 3
- key_gain: float32 [128], replicated, may hold values from 1.2 to 3
- text_keys: bfloat16 [2048, 1536], P('batch', 'tensor'), parts along dimension 0, may hold values from -12 to 12
- text_values: bfloat16 [2048, 1536], P('batch', 'tensor'), parts along dimension 0, may hold values from -6 to 6
- stale_keys: bfloat16 [32768, 1536], P(('batch', 'patch'), 'tensor'), parts along dimension 0, may hold values from -48 to 48, as said below
- stale_values: bfloat16 [32768, 1536], P(('batch', 'patch'), 'tensor'), parts along dimension 0, may hold values from -6 to 6
Outputs:
- update: bfloat16 [32768, 3072], P(('batch', 'patch'), 'tensor'), parts along dimension 0
The draws below stay inside these ranges and needn't reach their ends.
There are 4 independent parts, one for each index of `batch`. The reference program is written for one: setup_inputs(seed, part) draws one part's arguments, and reference() takes and returns one part's arrays. A program takes and returns all parts, laid end to end along the dimension named above; an argument that names none is the same for every part. Nothing has to cross between parts.
Inputs may be any that keep to these rules, and one draw needn't show every extreme that they name: `stale_keys`: cached keys of the previous step.
All inputs are finite; a program needn't handle non-finite values.
Results may differ from the reference program's by a relative error of at most 0.017.
Values may be sent and summed in bfloat16 or wider, within the bound.
A program may use at most 128 MiB of HBM per device.

```python
import math
import jax
import jax.numpy as jnp
from jax import lax

D = 3072
HEADS = 12
HEAD_DIM = 128
TEXT = 512
TOK_DEV = 512
IMG = 8192
N_PATCH = 16


def draw_stale_keys(key, part):
    key = jax.random.fold_in(key, 7)
    key_base = jax.random.fold_in(key, 1)
    dims = (IMG, HEADS * HEAD_DIM)
    drawn = jnp.clip(jax.random.normal(key_base, dims, jnp.float32) * 2.0, -12.0, 12.0)
    return drawn.astype(jnp.bfloat16)


def steps_of(stream_key, shape, pieces, smallest, high):
    loudness = 1.0
    for dim, parts in pieces:
        draws = jax.random.uniform(jax.random.fold_in(jax.random.fold_in(stream_key, 6), dim), (parts,), jnp.float32, smallest / len(pieces), high / len(pieces))
        loudness = loudness * jnp.repeat(jnp.exp(draws), shape[dim] // parts).reshape((-1,) + (1,) * (len(shape) - 1 - dim))
    return loudness


def normal_values(key, shape, spread, bound, cuts=(), kind=jnp.bfloat16):
    factor_of = steps_of(key, shape, cuts, -0.22, 0.18) if cuts else 1.0
    values = jax.random.normal(key, shape, jnp.float32) * spread * factor_of
    return jnp.minimum(jnp.maximum(values, -bound), bound).astype(kind)


def setup_inputs(seed: int = 0, part: int = 0) -> dict:
    keys = jax.random.split(jax.random.key(seed), 13)
    part_keys = jax.random.split(jax.random.fold_in(keys[12], part), 13)
    image = normal_values(part_keys[0], (IMG, D), 1.0, 6.0, ((0, 16), (1, 4)))
    modulation = normal_values(part_keys[1], (3, D), 0.7, 4.0, (), jnp.float32)
    w_query = normal_values(keys[2], (D, HEADS * HEAD_DIM), D ** -0.5, 0.109375, ((1, 4),))
    w_key = normal_values(keys[3], (D, HEADS * HEAD_DIM), D ** -0.5, 0.109375, ((1, 4),))
    w_value = normal_values(keys[4], (D, HEADS * HEAD_DIM), D ** -0.5, 0.109375, ((1, 4),))
    w_out = normal_values(keys[5], (HEADS * HEAD_DIM, D), (HEADS * HEAD_DIM) ** -0.5, 0.15625, ((0, 4),))
    query_gain = jnp.clip(jnp.exp(jax.random.uniform(keys[6], (HEAD_DIM,), jnp.float32, math.log(1.2), math.log(3.0))), 1.2, 3.0)
    key_gain = jnp.clip(jnp.exp(jax.random.uniform(keys[7], (HEAD_DIM,), jnp.float32, math.log(1.2), math.log(3.0))), 1.2, 3.0)
    text_keys = normal_values(part_keys[8], (TEXT, HEADS * HEAD_DIM), 2.0, 12.0, ((1, 4),))
    text_values = normal_values(part_keys[9], (TEXT, HEADS * HEAD_DIM), 1.0, 6.0, ((1, 4),))
    stale_keys = draw_stale_keys(jax.random.fold_in(jax.random.fold_in(keys[12], part), 71), part)
    stale_values = normal_values(part_keys[11], (IMG, HEADS * HEAD_DIM), 1.0, 6.0, ((0, 16), (1, 4)))
    return {"image": image, "modulation": modulation, "w_query": w_query, "w_key": w_key, "w_value": w_value, "w_out": w_out, "query_gain": query_gain, "key_gain": key_gain, "text_keys": text_keys, "text_values": text_values, "stale_keys": stale_keys, "stale_values": stale_values}


def modulate(image, modulation):
    values = image.astype(jnp.float32)
    row_mean = lax.optimization_barrier(jnp.mean(values, axis=-1, keepdims=True))
    centred = values - row_mean
    variance = lax.optimization_barrier(jnp.mean(centred * centred, axis=-1, keepdims=True))
    normed = centred * lax.rsqrt(variance + 1e-06)
    return (normed * (1.0 + modulation[1]) + modulation[0]).astype(jnp.bfloat16)

def head_norm(projected, gain, head_width):
    heads_view = projected.reshape(projected.shape[0], -1, head_width)
    power = lax.optimization_barrier(jnp.mean(heads_view * heads_view, axis=-1, keepdims=True))
    return (heads_view * lax.rsqrt(power + 1e-06) * gain).astype(jnp.bfloat16)

def reference(image, modulation, w_query, w_key, w_value, w_out, query_gain, key_gain, text_keys, text_values, stale_keys, stale_values):
    modulated = modulate(image, modulation)
    query = head_norm(jnp.dot(modulated, w_query, preferred_element_type=jnp.float32), query_gain, HEAD_DIM)
    fresh_keys = head_norm(jnp.dot(modulated, w_key, preferred_element_type=jnp.float32), key_gain, HEAD_DIM).reshape(IMG, HEADS * HEAD_DIM)
    fresh_values = jnp.dot(modulated, w_value, preferred_element_type=jnp.float32).astype(jnp.bfloat16)
    owners = jnp.arange(IMG, dtype=jnp.int32) // TOK_DEV
    score_scale = 1.0 / math.sqrt(HEAD_DIM)

    def attend(block_index):
        queries_here = lax.dynamic_slice_in_dim(query, (block_index * TOK_DEV).astype(jnp.int32), TOK_DEV, 0).astype(jnp.float32)
        own_rows = (owners == block_index)[:, None]
        image_keys = jnp.where(own_rows, fresh_keys, stale_keys)
        image_values = jnp.where(own_rows, fresh_values, stale_values)
        all_keys = jnp.concatenate([text_keys, image_keys], 0).reshape(-1, HEADS, HEAD_DIM).astype(jnp.float32)
        all_values = jnp.concatenate([text_values, image_values], 0).reshape(-1, HEADS, HEAD_DIM).astype(jnp.float32)
        scores = jnp.einsum('qhd,khd->hqk', queries_here, all_keys) * score_scale
        largest = lax.optimization_barrier(jnp.max(scores, axis=-1, keepdims=True))
        expo = jnp.exp(scores - largest)
        total = lax.optimization_barrier(jnp.sum(expo, axis=-1))
        weights = lax.optimization_barrier(expo.astype(jnp.bfloat16)).astype(jnp.float32)
        mixed = jnp.einsum('hqk,khd->hqd', weights, all_values) / total[..., None]
        return jnp.transpose(mixed, (1, 0, 2)).reshape(TOK_DEV, HEADS * HEAD_DIM).astype(jnp.bfloat16)
    attended = lax.map(attend, jnp.arange(N_PATCH, dtype=jnp.int32)).reshape(IMG, HEADS * HEAD_DIM)
    projected = jnp.dot(attended, w_out, preferred_element_type=jnp.float32)
    return (modulation[2] * projected).astype(jnp.bfloat16)
```

```python
import functools
import math

import jax
import jax.numpy as jnp
from jax import lax
from jax.experimental import pallas as pl
from jax.experimental.pallas import tpu as pltpu
from jax.sharding import PartitionSpec as P

MESH = pl.DeviceIdType.MESH
BF = jnp.bfloat16
F32 = jnp.float32
ROWS = 512
HW = 128
HEADS = 3
WIDE = HEADS * HW
SLICE = 768
DM = 4 * SLICE
CH = 128
NCH = ROWS // CH
KB = 2048
PIECES = 2
LOG2E = 1.4426950408889634

KV_NEAR = 0
KV_TWO = KV_NEAR + 4
KV_SIB = KV_TWO + 2
KV_Z = KV_SIB + 8
KV_FX = KV_Z + 2 * PIECES
KV_FTWO = KV_FX + 4 * PIECES
KV_FSIB = KV_FTWO + 2 * PIECES
W_A = KV_FSIB + 8 * PIECES
W_B = W_A + 3
W_C = W_B + 3
W_D = W_C + 3
O_A = W_D + 1
O_B = O_A + 4
O_C = O_B + 3
O_D = O_C + 3
IMG = O_D + 1
QKV = IMG + 4 * NCH
TAIL = QKV + 3 * NCH
OUT = TAIL + 4 * NCH
NSEM = OUT + NCH


def kernel(
    img_h, mod, wq_h, wk_h, wv_h, wo_h, qgain, kgain, tk_h, tv_h, sk_h, sv_h,
    out,
    kbuf, vbuf, img, w_own, w_end, w_o, modl, qbuf, stage, att, ostage, m_s, acc_s,
    ssem, rsem, lsem,
):
    yy = lax.axis_index("batch")
    patch = lax.axis_index("patch")
    t = lax.axis_index("tensor")
    zh = patch // 8
    xx = lax.rem(patch, 8) // 2
    cc = lax.rem(patch, 2)
    is_mid = (t == 1) | (t == 2)
    is_end = (t == 0) | (t == 3)
    pair = jnp.where(t < 2, 1 - t, 5 - t)

    def at_x(d):
        return {"patch": zh * 8 + lax.rem(xx + d + 4, 4) * 2 + cc}

    def at_y(d):
        return {"batch": lax.rem(yy + d + 4, 4)}

    sib = {"patch": zh * 8 + xx * 2 + (1 - cc)}
    far = {"patch": (1 - zh) * 8 + xx * 2 + cc}
    to_pair = {"tensor": pair}

    def copy(src, dst, i, dev):
        return pltpu.make_async_remote_copy(
            src_ref=src, dst_ref=dst, send_sem=ssem.at[i], recv_sem=rsem.at[i],
            device_id=dev, device_id_type=MESH,
        )

    def got(dst, i):
        copy(dst, dst, i, sib).wait_recv()

    def sent(src, i):
        copy(src, src, i, sib).wait_send()

    def block(buf, slot, piece=0, pieces=1):
        n = ROWS // pieces
        return buf.at[pl.ds(slot * ROWS + piece * n, n)]

    local = [
        pltpu.make_async_copy(wq_h, w_own.at[0], lsem.at[0]),
        pltpu.make_async_copy(wk_h, w_own.at[1], lsem.at[1]),
        pltpu.make_async_copy(wv_h, w_own.at[2], lsem.at[2]),
        pltpu.make_async_copy(tk_h, block(kbuf, 0), lsem.at[3]),
        pltpu.make_async_copy(tv_h, block(vbuf, 0), lsem.at[4]),
        pltpu.make_async_copy(img_h, img.at[t], lsem.at[5]),
    ]
    my_cols = pl.ds(pl.multiple_of(t * SLICE, SLICE), SLICE)
    pair_cols = pl.ds(pl.multiple_of(pair * SLICE, SLICE), SLICE)
    local_o = [
        pltpu.make_async_copy(wo_h.at[:, my_cols], w_o.at[0, :, pl.ds(0, SLICE)], lsem.at[6]),
        pltpu.make_async_copy(wo_h.at[:, pair_cols], w_o.at[0, :, pl.ds(SLICE, SLICE)], lsem.at[7]),
    ]

    peers = [sib, far] + [at_x(d) for d in (1, 2, 3)] + [at_y(d) for d in (1, 2, 3)]
    peers += [{"tensor": lax.rem(t + d, 4)} for d in (1, 2, 3)]
    barrier = pltpu.get_barrier_semaphore()
    for p in peers:
        pl.semaphore_signal(barrier, inc=1, device_id=p, device_id_type=MESH)
    pl.semaphore_wait(barrier, len(peers))

    stale = (sk_h, sv_h)
    bufs = (kbuf, vbuf)

    def z_piece(j, p):
        n = ROWS // PIECES
        return copy(
            stale[j].at[pl.ds(p * n, n)], block(bufs[j], 8, p, PIECES), KV_Z + j * PIECES + p, far
        )

    for p in range(PIECES):
        for j in range(2):
            z_piece(j, p).start()

    w_rows = pl.ds(pl.multiple_of(cc * 1536 + yy * 384 + xx * 96, 96), 96)

    def w_a(j):
        return copy((wq_h, wk_h, wv_h)[j].at[w_rows], w_end.at[j, w_rows], W_A + j, to_pair)

    @pl.when(is_end)
    def _():
        for j in range(3):
            w_a(j).start()

    def img_copy(m, c):
        r = lax.rem(t - m + 4, 4)
        rows = pl.ds(pl.multiple_of(c * CH, CH), CH)
        return copy(img_h.at[rows], img.at[t, rows], IMG + r * NCH + c, {"tensor": jnp.int32(m)})

    def start_img(c):
        for m in (1, 2):
            @pl.when(t != m)
            def _(m=m):
                img_copy(m, c).start()

    for c in range(NCH):
        start_img(c)

    for j in range(2):
        copy(stale[j], block(bufs[j], 2), KV_NEAR + 2 * j, at_x(-1)).start()
        copy(stale[j], block(bufs[j], 4), KV_NEAR + 2 * j + 1, at_x(1)).start()
    for j in range(2):
        copy(stale[j], block(bufs[j], 1), KV_SIB + 4 * j, sib).start()

    for cp in local:
        cp.start()

    @pl.when(is_mid)
    def _():
        for cp in local_o:
            cp.start()

    o_rows = pl.ds(pl.multiple_of(cc * 192 + yy * 48, 48), 48)
    o_cols = pl.ds(pl.multiple_of(xx * 384, 384), 384)

    def o_a(m):
        r = lax.rem(t - m + 4, 4)
        e = 3 * (m - 1)
        start = jnp.where(xx < 2, m, e) * SLICE + lax.rem(xx, 2) * 384
        src = wo_h.at[o_rows, pl.ds(pl.multiple_of(start, 384), 384)]
        return copy(src, w_o.at[r, o_rows, o_cols], O_A + r, {"tensor": jnp.int32(m)})

    for m in (1, 2):
        @pl.when(t != m)
        def _(m=m):
            o_a(m).start()

    m_s[...] = jnp.full(m_s.shape, -1e30, F32)
    acc_s[...] = jnp.zeros(acc_s.shape, F32)

    def w_b(d):
        piece = w_end.at[:, w_rows]
        return copy(piece, piece, W_B + d - 1, at_x(d))

    def w_c(d):
        rows = pl.ds(pl.multiple_of(cc * 1536 + yy * 384, 384), 384)
        piece = w_end.at[:, rows]
        return copy(piece, piece, W_C + d - 1, at_y(d))

    def w_d():
        piece = w_end.at[:, pl.ds(pl.multiple_of(cc * 1536, 1536), 1536)]
        return copy(piece, piece, W_D, sib)

    def o_b(d):
        piece = w_o.at[pl.ds(1, 3), o_rows, o_cols]
        return copy(piece, piece, O_B + d - 1, at_x(d))

    def o_c(d):
        piece = w_o.at[pl.ds(1, 3), o_rows]
        return copy(piece, piece, O_C + d - 1, at_y(d))

    def o_d():
        piece = w_o.at[pl.ds(1, 3), pl.ds(pl.multiple_of(cc * 192, 192), 192)]
        return copy(piece, piece, O_D, sib)

    def wait_w_b():
        for d in (1, 2, 3):
            rows = pl.ds(pl.multiple_of(cc * 1536 + yy * 384 + lax.rem(xx - d + 4, 4) * 96, 96), 96)
            got(w_end.at[:, rows], W_B + d - 1)

    def wait_w_c():
        for d in (1, 2, 3):
            rows = pl.ds(pl.multiple_of(cc * 1536 + lax.rem(yy - d + 4, 4) * 384, 384), 384)
            got(w_end.at[:, rows], W_C + d - 1)

    def wait_o_b():
        for d in (1, 2, 3):
            cols = pl.ds(pl.multiple_of(lax.rem(xx - d + 4, 4) * 384, 384), 384)
            got(w_o.at[pl.ds(1, 3), o_rows, cols], O_B + d - 1)

    def wait_o_c():
        for d in (1, 2, 3):
            rows = pl.ds(pl.multiple_of(cc * 192 + lax.rem(yy - d + 4, 4) * 48, 48), 48)
            got(w_o.at[pl.ds(1, 3), rows], O_C + d - 1)

    @pl.when(is_mid)
    def _():
        for j in range(3):
            got(w_end.at[j, w_rows], W_A + j)
        for d in (1, 2, 3):
            w_b(d).start()
        for r in (1, 2, 3):
            got(w_o.at[r, o_rows, o_cols], O_A + r)
        for d in (1, 2, 3):
            o_b(d).start()

    def near_sib(j, i):
        src = stale[j] if i == 0 else block(bufs[j], 2 * i)
        return copy(src, block(bufs[j], 2 * i + 1), KV_SIB + 4 * j + i, sib)

    def near_two(j):
        if j == 0:
            return copy(block(kbuf, 4), block(kbuf, 6), KV_TWO, at_x(1))
        return copy(block(vbuf, 2), block(vbuf, 6), KV_TWO + 1, at_x(-1))

    @pl.when(is_mid)
    def _():
        wait_w_b()
        for d in (1, 2, 3):
            w_c(d).start()
        wait_o_b()
        for d in (1, 2, 3):
            o_c(d).start()

    got(block(kbuf, 4), KV_NEAR + 1)
    near_two(0).start()
    got(block(vbuf, 2), KV_NEAR + 2)
    near_two(1).start()
    near_sib(0, 2).start()
    near_sib(1, 1).start()
    got(block(kbuf, 2), KV_NEAR)
    near_sib(0, 1).start()
    got(block(vbuf, 4), KV_NEAR + 3)
    near_sib(1, 2).start()

    @pl.when(is_mid)
    def _():
        wait_w_c()
        w_d().start()
        wait_o_c()
        o_d().start()

    def far_x(j, p, s):
        src = block(bufs[j], 8, p, PIECES)
        dst = block(bufs[j], 10 + 2 * s, p, PIECES)
        return copy(src, dst, KV_FX + (j * PIECES + p) * 2 + s, at_x(-1 if s == 0 else 1))

    def far_two(j, p):
        src = block(bufs[j], 12 if j == 0 else 10, p, PIECES)
        dst = block(bufs[j], 14, p, PIECES)
        return copy(src, dst, KV_FTWO + j * PIECES + p, at_x(1 if j == 0 else -1))

    def far_sib(j, p, i):
        src = block(bufs[j], 8 + 2 * i, p, PIECES)
        dst = block(bufs[j], 9 + 2 * i, p, PIECES)
        return copy(src, dst, KV_FSIB + (j * PIECES + p) * 4 + i, sib)

    for p in range(PIECES):
        for j in range(2):
            got(block(bufs[j], 8, p, PIECES), KV_Z + j * PIECES + p)
            far_x(j, p, 0).start()
            far_x(j, p, 1).start()
            far_sib(j, p, 0).start()

    for j in range(2):
        got(block(bufs[j], 6), KV_TWO + j)
        near_sib(j, 3).start()

    def far_rest():
        for p in range(PIECES):
            for j in range(2):
                for s in (0, 1):
                    got(block(bufs[j], 10 + 2 * s, p, PIECES), KV_FX + (j * PIECES + p) * 2 + s)
                far_two(j, p).start()
                far_sib(j, p, 1).start()
                far_sib(j, p, 2).start()
        for p in range(PIECES):
            for j in range(2):
                got(block(bufs[j], 14, p, PIECES), KV_FTWO + j * PIECES + p)
                far_sib(j, p, 3).start()
        for p in range(PIECES):
            for j in range(2):
                for i in range(4):
                    got(
                        block(bufs[j], 9 + 2 * i, p, PIECES),
                        KV_FSIB + (j * PIECES + p) * 4 + i,
                    )

    def near_rest():
        for j in range(2):
            for i in range(4):
                got(block(bufs[j], 2 * i + 1), KV_SIB + 4 * j + i)

    def chunk_rows(c, base=0):
        return pl.ds(pl.multiple_of(base + c * CH, CH), CH)

    def norm_chunk(c):
        rows = chunk_rows(c)
        total = jnp.zeros((CH, 1), F32)
        for s in range(4):
            total += jnp.sum(img[s, rows].astype(F32), axis=1, keepdims=True)
        mean = total * (1.0 / DM)
        total = jnp.zeros((CH, 1), F32)
        for s in range(4):
            d = img[s, rows].astype(F32) - mean
            total += jnp.sum(d * d, axis=1, keepdims=True)
        rstd = lax.rsqrt(total * (1.0 / DM) + 1e-06)
        for s in range(4):
            cols = slice(s * SLICE, (s + 1) * SLICE)
            d = (img[s, rows].astype(F32) - mean) * rstd
            modl[:, cols] = (d * (1.0 + mod[1:2, cols]) + mod[0:1, cols]).astype(BF)

    def project(w, put):
        for j in range(3):
            y = jnp.dot(modl[...], w[j], preferred_element_type=F32)
            if j == 2:
                put(j, y.astype(BF))
                continue
            gain = qgain[...] * (LOG2E / math.sqrt(HW)) if j == 0 else kgain[...]
            parts = []
            for h in range(HEADS):
                v = y[:, h * HW : (h + 1) * HW]
                power = jnp.mean(v * v, axis=1, keepdims=True)
                parts.append((v * lax.rsqrt(power + 1e-06) * gain).astype(BF))
            put(j, jnp.concatenate(parts, axis=1))

    FRESH = 16 * ROWS

    def qkv_copy(j, c):
        dst = (
            qbuf.at[chunk_rows(c)],
            kbuf.at[chunk_rows(c, FRESH)],
            vbuf.at[chunk_rows(c, FRESH)],
        )[j]
        return copy(stage.at[j, chunk_rows(c)], dst, QKV + j * NCH + c, to_pair)

    def fresh_chunk(c):
        @pl.when(is_mid)
        def _():
            for r in (1, 2, 3):
                s = lax.rem(t + r, 4)
                got(img.at[s, chunk_rows(c)], IMG + r * NCH + c)
            norm_chunk(c)

            def put_end(j, v):
                stage[j, chunk_rows(c)] = v
                qkv_copy(j, c).start()

            project(w_end, put_end)

            def put_own(j, v):
                if j == 0:
                    qbuf[chunk_rows(c)] = v
                else:
                    bufs[j - 1][chunk_rows(c, FRESH)] = v

            project(w_own, put_own)

        @pl.when(is_end)
        def _():
            got(qbuf.at[chunk_rows(c)], QKV + c)
            got(kbuf.at[chunk_rows(c, FRESH)], QKV + NCH + c)
            got(vbuf.at[chunk_rows(c, FRESH)], QKV + 2 * NCH + c)

    def attend(c, start, n):
        rows = chunk_rows(c)
        keys = pl.ds(pl.multiple_of(start, ROWS), n)
        for h in range(HEADS):
            cols = slice(h * HW, (h + 1) * HW)
            k = kbuf[keys, cols]
            v = vbuf[keys, cols]
            s = lax.dot_general(
                qbuf[rows, cols], k, (((1,), (1,)), ((), ())), preferred_element_type=F32
            )
            old = m_s[h, rows]
            new = jnp.maximum(old, jnp.max(s, axis=1, keepdims=True))
            shrink = jnp.exp2(old - new)
            p = jnp.exp2(s - new[:, :1]).astype(BF)
            m_s[h, rows] = new
            both = jnp.concatenate([v, jnp.ones_like(v)], axis=1)
            pv = jnp.dot(p, both, preferred_element_type=F32)
            acc_s[h, rows] = acc_s[h, rows] * jnp.concatenate([shrink, shrink], axis=1) + pv

    def tail_copy(m, c):
        r = lax.rem(t - m + 4, 4)
        rows = chunk_rows(c)
        return copy(att.at[0, rows], att.at[r, rows], TAIL + r * NCH + c, {"tensor": jnp.int32(m)})

    def finish(c):
        attend(c, FRESH, ROWS)
        rows = chunk_rows(c)
        for h in range(HEADS):
            a = acc_s[h, rows]
            att[0, rows, h * HW : (h + 1) * HW] = (a[:, :HW] / a[:, HW:]).astype(BF)
        for m in (1, 2):
            @pl.when(t != m)
            def _(m=m):
                tail_copy(m, c).start()

    for cp in local:
        cp.wait()

    @pl.when(is_mid)
    def _():
        for cp in local_o:
            cp.wait()
        got(w_end.at[:, pl.ds(pl.multiple_of((1 - cc) * 1536, 1536), 1536)], W_D)
        got(w_o.at[pl.ds(1, 3), pl.ds(pl.multiple_of((1 - cc) * 192, 192), 192)], O_D)

    @pl.loop(0, NCH)
    def _(c):
        fresh_chunk(c)

        @pl.when(c == 0)
        def _():
            near_rest()

        @pl.when(c == NCH - 1)
        def _():
            @pl.loop(0, NCH - 1)
            def _(d):
                finish(d)

        @pl.loop(0, 4096 // KB)
        def _(b):
            attend(c, b * KB, KB)

        @pl.when(c == 0)
        def _():
            far_rest()

        @pl.loop(4096 // KB, 8192 // KB)
        def _(b):
            attend(c, b * KB, KB)

    finish(NCH - 1)

    def out_copy(c):
        return copy(ostage.at[chunk_rows(c)], out.at[chunk_rows(c)], OUT + c, to_pair)

    @pl.when(is_mid)
    def _():
        gate_own = mod[2:3, my_cols]
        gate_end = mod[2:3, pair_cols]

        @pl.loop(0, NCH)
        def _(c):
            rows = chunk_rows(c)
            for r in (1, 2, 3):
                got(att.at[r, rows], TAIL + r * NCH + c)
            for half, gate in ((1, gate_end), (0, gate_own)):
                y = jnp.zeros((CH, SLICE), F32)
                for r in range(4):
                    w = w_o[r, :, half * SLICE : (half + 1) * SLICE]
                    y += jnp.dot(att[r, rows], w, preferred_element_type=F32)
                y = (y * gate).astype(BF)
                if half:
                    ostage[rows] = y
                    out_copy(c).start()
                else:
                    out[rows] = y

    @pl.when(is_end)
    def _():
        for c in range(NCH):
            got(out.at[chunk_rows(c)], OUT + c)

    for j in range(2):
        for p in range(PIECES):
            z_piece(j, p).wait_send()
            far_two(j, p).wait_send()
            for s in range(2):
                far_x(j, p, s).wait_send()
            for i in range(4):
                far_sib(j, p, i).wait_send()
        for s in range(2):
            sent(stale[j], KV_NEAR + 2 * j + s)
        for i in range(4):
            near_sib(j, i).wait_send()
        near_two(j).wait_send()

    @pl.when(is_end)
    def _():
        for j in range(3):
            w_a(j).wait_send()

    for m in (1, 2):
        @pl.when(t != m)
        def _(m=m):
            o_a(m).wait_send()
            for c in range(NCH):
                img_copy(m, c).wait_send()
                tail_copy(m, c).wait_send()

    @pl.when(is_mid)
    def _():
        for d in (1, 2, 3):
            w_b(d).wait_send()
            w_c(d).wait_send()
            o_b(d).wait_send()
            o_c(d).wait_send()
        w_d().wait_send()
        o_d().wait_send()
        for c in range(NCH):
            out_copy(c).wait_send()
            for j in range(3):
                qkv_copy(j, c).wait_send()


def shards(image, modulation, w_query, w_key, w_value, w_out, query_gain, key_gain, text_keys, text_values, stale_keys, stale_values):
    hbm = pl.BlockSpec(memory_space=pl.ANY)
    vmem = pl.BlockSpec(memory_space=pltpu.VMEM)
    return pl.pallas_call(
        kernel,
        out_shape=jax.ShapeDtypeStruct((ROWS, SLICE), BF),
        in_specs=[hbm, vmem, hbm, hbm, hbm, hbm, vmem, vmem, hbm, hbm, hbm, hbm],
        out_specs=vmem,
        scratch_shapes=[
            pltpu.VMEM((17 * ROWS, WIDE), BF),
            pltpu.VMEM((17 * ROWS, WIDE), BF),
            pltpu.VMEM((4, ROWS, SLICE), BF),
            pltpu.VMEM((3, DM, WIDE), BF),
            pltpu.VMEM((3, DM, WIDE), BF),
            pltpu.VMEM((4, WIDE, 2 * SLICE), BF),
            pltpu.VMEM((CH, DM), BF),
            pltpu.VMEM((ROWS, WIDE), BF),
            pltpu.VMEM((3, ROWS, WIDE), BF),
            pltpu.VMEM((4, ROWS, WIDE), BF),
            pltpu.VMEM((ROWS, SLICE), BF),
            pltpu.VMEM((HEADS, ROWS, HW), F32),
            pltpu.VMEM((HEADS, ROWS, 2 * HW), F32),
            pltpu.SemaphoreType.DMA((NSEM,)),
            pltpu.SemaphoreType.DMA((NSEM,)),
            pltpu.SemaphoreType.DMA((8,)),
        ],
        compiler_params=pltpu.CompilerParams(
            collective_id=0, has_side_effects=True, vmem_limit_bytes=60 * 1024 * 1024
        ),
        cost_estimate=pl.CostEstimate(
            flops=12_000_000_000, bytes_accessed=20_000_000, transcendentals=14_000_000
        ),
        name="joint_attention",
    )(
        image, modulation, w_query, w_key, w_value, w_out,
        query_gain.reshape(1, HW), key_gain.reshape(1, HW),
        text_keys, text_values, stale_keys, stale_values,
    )


def solution(mesh):
    rows = P(("batch", "patch"), "tensor")
    cols = P(None, "tensor")
    in_specs = (
        rows, P("batch", None), cols, cols, cols, P("tensor", None), P(), P(),
        P("batch", "tensor"), P("batch", "tensor"), rows, rows,
    )
    return jax.shard_map(shards, mesh=mesh, in_specs=in_specs, out_specs=rows, check_vma=False)
```

```python
import functools
import math

import jax
import jax.numpy as jnp
from jax import lax
from jax.experimental import pallas as pl
from jax.experimental.pallas import tpu as pltpu
from jax.sharding import PartitionSpec as P

MESH = pl.DeviceIdType.MESH
BF = jnp.bfloat16
F32 = jnp.float32
ROWS = 512
HW = 128
HEADS = 3
WIDE = HEADS * HW
SLICE = 768
DM = 4 * SLICE
CH = 128
NCH = ROWS // CH
KB = 2048
PIECES = 2
LOG2E = 1.4426950408889634

KV_NEAR = 0
KV_TWO = KV_NEAR + 4
KV_SIB = KV_TWO + 2
KV_Z = KV_SIB + 8
KV_FX = KV_Z + 2 * PIECES
KV_FTWO = KV_FX + 4 * PIECES
KV_FSIB = KV_FTWO + 2 * PIECES
W_A = KV_FSIB + 8 * PIECES
W_B = W_A + 3
W_C = W_B + 3
W_D = W_C + 12
O_A = W_D + 3
O_B = O_A + 4
O_C = O_B + 3
O_D = O_C + 3
IMG = O_D + 1
QKV = IMG + 4 * NCH
TAIL = QKV + 3 * NCH
OUT = TAIL + 4 * NCH
NSEM = OUT + NCH


def kernel(
    img_h, mod, wq_h, wk_h, wv_h, wo_h, qgain, kgain, tk_h, tv_h, sk_h, sv_h,
    out,
    kbuf, vbuf, img, w_own, w_end, w_o, modl, qbuf, stage, att, ostage, m_s, acc_s,
    ssem, rsem, lsem,
):
    yy = lax.axis_index("batch")
    patch = lax.axis_index("patch")
    t = lax.axis_index("tensor")
    zh = patch // 8
    xx = lax.rem(patch, 8) // 2
    cc = lax.rem(patch, 2)
    is_mid = (t == 1) | (t == 2)
    is_end = (t == 0) | (t == 3)
    pair = jnp.where(t < 2, 1 - t, 5 - t)

    def at_x(d):
        return {"patch": zh * 8 + lax.rem(xx + d + 4, 4) * 2 + cc}

    def at_y(d):
        return {"batch": lax.rem(yy + d + 4, 4)}

    sib = {"patch": zh * 8 + xx * 2 + (1 - cc)}
    far = {"patch": (1 - zh) * 8 + xx * 2 + cc}
    to_pair = {"tensor": pair}

    def copy(src, dst, base, off, dev):
        i = base + off
        return pltpu.make_async_remote_copy(
            src_ref=src, dst_ref=dst, send_sem=ssem.at[i], recv_sem=rsem.at[i],
            device_id=dev, device_id_type=MESH,
        )

    def got(dst, base, off=0):
        copy(dst, dst, base, off, sib).wait_recv()

    def block(buf, slot, piece=0, pieces=1):
        n = ROWS // pieces
        return buf.at[pl.ds(slot * ROWS + piece * n, n)]

    local = [
        pltpu.make_async_copy(wq_h, w_own.at[0], lsem.at[0]),
        pltpu.make_async_copy(wk_h, w_own.at[1], lsem.at[1]),
        pltpu.make_async_copy(wv_h, w_own.at[2], lsem.at[2]),
        pltpu.make_async_copy(tk_h, block(kbuf, 0), lsem.at[3]),
        pltpu.make_async_copy(tv_h, block(vbuf, 0), lsem.at[4]),
        pltpu.make_async_copy(img_h, img.at[t], lsem.at[5]),
    ]
    my_cols = pl.ds(pl.multiple_of(t * SLICE, SLICE), SLICE)
    pair_cols = pl.ds(pl.multiple_of(pair * SLICE, SLICE), SLICE)
    local_o = [
        pltpu.make_async_copy(wo_h.at[:, my_cols], w_o.at[0, :, pl.ds(0, SLICE)], lsem.at[6]),
        pltpu.make_async_copy(wo_h.at[:, pair_cols], w_o.at[0, :, pl.ds(SLICE, SLICE)], lsem.at[7]),
    ]

    for cp in local:
        cp.start()

    @pl.when(is_mid)
    def _():
        for cp in local_o:
            cp.start()

    peers = [sib, far] + [at_x(d) for d in (1, 2, 3)] + [at_y(d) for d in (1, 2, 3)]
    peers += [{"tensor": lax.rem(t + d, 4)} for d in (1, 2, 3)]
    barrier = pltpu.get_barrier_semaphore()
    for p in peers:
        pl.semaphore_signal(barrier, inc=1, device_id=p, device_id_type=MESH)
    pl.semaphore_wait(barrier, len(peers))

    stale = (sk_h, sv_h)
    bufs = (kbuf, vbuf)

    def z_piece(j, p):
        n = ROWS // PIECES
        return copy(
            stale[j].at[pl.ds(p * n, n)], block(bufs[j], 8, p, PIECES), KV_Z, j * PIECES + p, far
        )

    w_rows = pl.ds(pl.multiple_of(cc * 1536 + yy * 384 + xx * 96, 96), 96)

    def w_a(j):
        return copy((wq_h, wk_h, wv_h)[j].at[w_rows], w_end.at[j, w_rows], W_A, j, to_pair)

    @pl.when(is_end)
    def _():
        for j in range(3):
            w_a(j).start()

    def img_copy(m, c):
        r = lax.rem(t - m + 4, 4)
        rows = pl.ds(pl.multiple_of(c * CH, CH), CH)
        return copy(img_h.at[rows], img.at[t, rows], IMG, r * NCH + c, {"tensor": jnp.int32(m)})

    def start_img(c):
        for m in (1, 2):
            @pl.when(t != m)
            def _(m=m):
                img_copy(m, c).start()

    o_rows = pl.ds(pl.multiple_of(cc * 192 + yy * 48, 48), 48)
    o_cols = pl.ds(pl.multiple_of(xx * 384, 384), 384)

    def o_a(m):
        r = lax.rem(t - m + 4, 4)
        e = 3 * (m - 1)
        start = jnp.where(xx < 2, m, e) * SLICE + lax.rem(xx, 2) * 384
        src = wo_h.at[o_rows, pl.ds(pl.multiple_of(start, 384), 384)]
        return copy(src, w_o.at[r, o_rows, o_cols], O_A, r, {"tensor": jnp.int32(m)})

    for m in (1, 2):
        @pl.when(t != m)
        def _(m=m):
            o_a(m).start()

    m_s[...] = jnp.full(m_s.shape, -1e30, F32)
    acc_s[...] = jnp.zeros(acc_s.shape, F32)

    def w_b(d):
        piece = w_end.at[:, w_rows]
        return copy(piece, piece, W_B, d - 1, at_x(d))

    def y_rows(d, half=None):
        n = 384 if half is None else 192
        first = cc * 1536 + lax.rem(yy + d + 4, 4) * 384 + (192 if half else 0)
        return pl.ds(pl.multiple_of(first, n), n)

    def w_c(j, s):
        piece = w_end.at[j, y_rows(0)]
        return copy(piece, piece, W_C, 2 * j + s, at_y(1 - 2 * s))

    def w_two(j, s):
        piece = w_end.at[j, y_rows(2 * s - 1, s)]
        return copy(piece, piece, W_C, 6 + 2 * j + s, at_y(1 - 2 * s))

    def w_d(j):
        piece = w_end.at[j, pl.ds(pl.multiple_of(cc * 1536, 1536), 1536)]
        return copy(piece, piece, W_D, j, sib)

    def w_forward(j):
        for s in (0, 1):
            got(w_end.at[j, y_rows(2 * s - 1)], W_C, 2 * j + s)
            w_two(j, s).start()

    def w_share(j):
        for s in (0, 1):
            got(w_end.at[j, y_rows(2, s)], W_C, 6 + 2 * j + s)
        w_d(j).start()

    def o_b(d):
        piece = w_o.at[pl.ds(1, 3), o_rows, o_cols]
        return copy(piece, piece, O_B, d - 1, at_x(d))

    def o_c(d):
        piece = w_o.at[pl.ds(1, 3), o_rows]
        return copy(piece, piece, O_C, d - 1, at_y(d))

    def o_d():
        piece = w_o.at[pl.ds(1, 3), pl.ds(pl.multiple_of(cc * 192, 192), 192)]
        return copy(piece, piece, O_D, 0, sib)

    def wait_w_b():
        for d in (1, 2, 3):
            rows = pl.ds(pl.multiple_of(cc * 1536 + yy * 384 + lax.rem(xx - d + 4, 4) * 96, 96), 96)
            got(w_end.at[:, rows], W_B, d - 1)

    def wait_o_b():
        for d in (1, 2, 3):
            cols = pl.ds(pl.multiple_of(lax.rem(xx - d + 4, 4) * 384, 384), 384)
            got(w_o.at[pl.ds(1, 3), o_rows, cols], O_B, d - 1)

    def wait_o_c():
        for d in (1, 2, 3):
            rows = pl.ds(pl.multiple_of(cc * 192 + lax.rem(yy - d + 4, 4) * 48, 48), 48)
            got(w_o.at[pl.ds(1, 3), rows], O_C, d - 1)

    def near_sib(j, i):
        src = stale[j] if i == 0 else block(bufs[j], 2 * i)
        return copy(src, block(bufs[j], 2 * i + 1), KV_SIB, 4 * j + i, sib)

    def near_two(j):
        if j == 0:
            return copy(block(kbuf, 4), block(kbuf, 6), KV_TWO, 0, at_x(1))
        return copy(block(vbuf, 2), block(vbuf, 6), KV_TWO, 1, at_x(-1))

    def far_x(j, p, s):
        src = block(bufs[j], 8, p, PIECES)
        dst = block(bufs[j], 10 + 2 * s, p, PIECES)
        return copy(src, dst, KV_FX, (j * PIECES + p) * 2 + s, at_x(-1 if s == 0 else 1))

    def far_two(j, p):
        src = block(bufs[j], 12 if j == 0 else 10, p, PIECES)
        dst = block(bufs[j], 14, p, PIECES)
        return copy(src, dst, KV_FTWO, j * PIECES + p, at_x(1 if j == 0 else -1))

    def far_sib(j, p, i):
        src = block(bufs[j], 8 + 2 * i, p, PIECES)
        dst = block(bufs[j], 9 + 2 * i, p, PIECES)
        return copy(src, dst, KV_FSIB, (j * PIECES + p) * 4 + i, sib)

    def far_z(j, p):
        got(block(bufs[j], 8, p, PIECES), KV_Z, j * PIECES + p)
        far_x(j, p, 0).start()
        far_x(j, p, 1).start()
        far_sib(j, p, 0).start()

    def far_on(p):
        for j in range(2):
            for s in (0, 1):
                got(block(bufs[j], 10 + 2 * s, p, PIECES), KV_FX, (j * PIECES + p) * 2 + s)
            far_two(j, p).start()
            far_sib(j, p, 1).start()
            far_sib(j, p, 2).start()

    def far_last():
        for p in range(PIECES):
            for j in range(2):
                got(block(bufs[j], 14, p, PIECES), KV_FTWO, j * PIECES + p)
                far_sib(j, p, 3).start()

    def far_rest():
        for p in range(PIECES):
            for j in range(2):
                for i in range(4):
                    got(
                        block(bufs[j], 9 + 2 * i, p, PIECES),
                        KV_FSIB, (j * PIECES + p) * 4 + i,
                    )

    def near_on():
        got(block(kbuf, 4), KV_NEAR, 1)
        near_two(0).start()
        got(block(vbuf, 2), KV_NEAR, 2)
        near_two(1).start()
        near_sib(0, 2).start()
        near_sib(1, 1).start()
        got(block(kbuf, 2), KV_NEAR)
        near_sib(0, 1).start()
        got(block(vbuf, 4), KV_NEAR, 3)
        near_sib(1, 2).start()

    def near_last():
        for j in range(2):
            got(block(bufs[j], 6), KV_TWO, j)
            near_sib(j, 3).start()

    def start_near():
        for j in range(2):
            copy(stale[j], block(bufs[j], 2), KV_NEAR, 2 * j, at_x(-1)).start()
            copy(stale[j], block(bufs[j], 4), KV_NEAR, 2 * j + 1, at_x(1)).start()

    for j in range(2):
        copy(stale[j], block(bufs[j], 1), KV_SIB, 4 * j, sib).start()

    @pl.when(is_end)
    def _():
        start_near()
        for j in range(3):
            w_a(j).wait_send()

    @pl.when(is_mid)
    def _():
        for j in range(3):
            got(w_end.at[j, w_rows], W_A, j)
        for d in (1, 2, 3):
            w_b(d).start()

    for m in (1, 2):
        @pl.when(t != m)
        def _(m=m):
            o_a(m).wait_send()

    @pl.when(is_mid)
    def _():
        for r in (1, 2, 3):
            got(w_o.at[r, o_rows, o_cols], O_A, r)

    for p in range(PIECES):
        for j in range(2):
            z_piece(j, p).start()

    for c in range(NCH):
        start_img(c)

    @pl.when(is_end)
    def _():
        far_z(0, 0)
        far_z(1, 0)
        near_on()
        far_z(0, 1)
        far_z(1, 1)
        far_on(0)
        near_last()
        far_on(1)
        far_last()

    @pl.when(is_mid)
    def _():
        wait_w_b()
        for j in range(3):
            for s in (0, 1):
                w_c(j, s).start()
        start_near()
        for d in (1, 2, 3):
            o_b(d).start()
        far_z(0, 0)
        w_forward(0)
        far_z(1, 0)
        w_forward(1)
        far_z(0, 1)
        far_z(1, 1)
        w_forward(2)
        near_on()
        far_on(0)
        wait_o_b()
        for d in (1, 2, 3):
            o_c(d).start()
        for j in range(3):
            w_share(j)
        near_last()

    def near_rest():
        for j in range(2):
            for i in range(4):
                got(block(bufs[j], 2 * i + 1), KV_SIB, 4 * j + i)

    def chunk_rows(c, base=0):
        return pl.ds(pl.multiple_of(base + c * CH, CH), CH)

    def norm_chunk(c):
        rows = chunk_rows(c)
        total = jnp.zeros((CH, 1), F32)
        for s in range(4):
            total += jnp.sum(img[s, rows].astype(F32), axis=1, keepdims=True)
        mean = total * (1.0 / DM)
        total = jnp.zeros((CH, 1), F32)
        for s in range(4):
            d = img[s, rows].astype(F32) - mean
            total += jnp.sum(d * d, axis=1, keepdims=True)
        rstd = lax.rsqrt(total * (1.0 / DM) + 1e-06)
        for s in range(4):
            cols = slice(s * SLICE, (s + 1) * SLICE)
            d = (img[s, rows].astype(F32) - mean) * rstd
            modl[:, cols] = (d * (1.0 + mod[1:2, cols]) + mod[0:1, cols]).astype(BF)

    def project(w, put):
        for j in range(3):
            y = jnp.dot(modl[...], w[j], preferred_element_type=F32)
            if j == 2:
                put(j, y.astype(BF))
                continue
            gain = qgain[...] * (LOG2E / math.sqrt(HW)) if j == 0 else kgain[...]
            parts = []
            for h in range(HEADS):
                v = y[:, h * HW : (h + 1) * HW]
                power = jnp.mean(v * v, axis=1, keepdims=True)
                parts.append((v * lax.rsqrt(power + 1e-06) * gain).astype(BF))
            put(j, jnp.concatenate(parts, axis=1))

    FRESH = 16 * ROWS

    def qkv_copy(j, c):
        dst = (
            qbuf.at[chunk_rows(c)],
            kbuf.at[chunk_rows(c, FRESH)],
            vbuf.at[chunk_rows(c, FRESH)],
        )[j]
        return copy(stage.at[j, chunk_rows(c)], dst, QKV, j * NCH + c, to_pair)

    def middle_chunk(c):
        for r in (1, 2, 3):
            s = lax.rem(t + r, 4)
            got(img.at[s, chunk_rows(c)], IMG, r * NCH + c)
        norm_chunk(c)

        def put_end(j, v):
            stage[j, chunk_rows(c)] = v
            qkv_copy(j, c).start()

        project(w_end, put_end)

        def put_own(j, v):
            if j == 0:
                qbuf[chunk_rows(c)] = v
            else:
                bufs[j - 1][chunk_rows(c, FRESH)] = v

        project(w_own, put_own)

    def end_chunk(c):
        got(qbuf.at[chunk_rows(c)], QKV, c)
        got(kbuf.at[chunk_rows(c, FRESH)], QKV, NCH + c)
        got(vbuf.at[chunk_rows(c, FRESH)], QKV, 2 * NCH + c)

    def fresh_chunk(c):
        @pl.when(is_mid)
        def _():
            middle_chunk(c)

        @pl.when(is_end)
        def _():
            end_chunk(c)

    def attend(c, start, n):
        rows = chunk_rows(c)
        keys = pl.ds(pl.multiple_of(start, ROWS), n)
        for h in range(HEADS):
            cols = slice(h * HW, (h + 1) * HW)
            k = kbuf[keys, cols]
            v = vbuf[keys, cols]
            s = lax.dot_general(
                qbuf[rows, cols], k, (((1,), (1,)), ((), ())), preferred_element_type=F32
            )
            old = m_s[h, rows]
            new = jnp.maximum(old, jnp.max(s, axis=1, keepdims=True))
            shrink = jnp.exp2(old - new)
            p = jnp.exp2(s - new[:, :1]).astype(BF)
            m_s[h, rows] = new
            both = jnp.concatenate([v, jnp.ones_like(v)], axis=1)
            pv = jnp.dot(p, both, preferred_element_type=F32)
            acc_s[h, rows] = acc_s[h, rows] * jnp.concatenate([shrink, shrink], axis=1) + pv

    def tail_copy(m, c):
        r = lax.rem(t - m + 4, 4)
        rows = chunk_rows(c)
        return copy(att.at[0, rows], att.at[r, rows], TAIL, r * NCH + c, {"tensor": jnp.int32(m)})

    def finish(c):
        attend(c, FRESH, ROWS)
        rows = chunk_rows(c)
        for h in range(HEADS):
            a = acc_s[h, rows]
            att[0, rows, h * HW : (h + 1) * HW] = (a[:, :HW] / a[:, HW:]).astype(BF)
        for m in (1, 2):
            @pl.when(t != m)
            def _(m=m):
                tail_copy(m, c).start()

    for cp in local:
        cp.wait()

    @pl.when(is_mid)
    def _():
        for cp in local_o:
            cp.wait()
        for j in range(3):
            rows = pl.ds(pl.multiple_of((1 - cc) * 1536, 1536), 1536)
            got(w_end.at[j, rows], W_D, j)

    def near(c):
        @pl.loop(0, 4096 // KB)
        def _(b):
            attend(c, b * KB, KB)

    def distant(c):
        @pl.loop(4096 // KB, 8192 // KB)
        def _(b):
            attend(c, b * KB, KB)

    @pl.loop(0, NCH - 1)
    def _(c):
        fresh_chunk(c)

        @pl.when(c == 0)
        def _():
            near_rest()

        near(c)
        @pl.when((c == 0) & is_mid)
        def _():
            far_on(1)

        @pl.when((c == 1) & is_mid)
        def _():
            far_last()

        @pl.when((c == NCH - 2) & is_mid)
        def _():
            wait_o_c()
            o_d().start()

    @pl.when(is_mid)
    def _():
        middle_chunk(NCH - 1)

    far_rest()

    @pl.loop(0, NCH - 1)
    def _(c):
        distant(c)

    @pl.when(is_end)
    def _():
        end_chunk(NCH - 1)

    @pl.loop(0, NCH - 1)
    def _(c):
        finish(c)

    @pl.loop(0, 8192 // KB)
    def _(b):
        attend(NCH - 1, b * KB, KB)

    finish(NCH - 1)

    @pl.when(is_mid)
    def _():
        got(w_o.at[pl.ds(1, 3), pl.ds(pl.multiple_of((1 - cc) * 192, 192), 192)], O_D)

    def out_copy(c):
        return copy(ostage.at[chunk_rows(c)], out.at[chunk_rows(c)], OUT, c, to_pair)

    @pl.when(is_mid)
    def _():
        gate_own = mod[2:3, my_cols]
        gate_end = mod[2:3, pair_cols]

        @pl.loop(0, NCH)
        def _(c):
            rows = chunk_rows(c)
            for r in (1, 2, 3):
                got(att.at[r, rows], TAIL, r * NCH + c)
            for half, gate in ((1, gate_end), (0, gate_own)):
                y = jnp.zeros((CH, SLICE), F32)
                for r in range(4):
                    w = w_o[r, :, half * SLICE : (half + 1) * SLICE]
                    y += jnp.dot(att[r, rows], w, preferred_element_type=F32)
                y = (y * gate).astype(BF)
                if half:
                    ostage[rows] = y
                    out_copy(c).start()
                else:
                    out[rows] = y

    @pl.when(is_end)
    def _():
        for c in range(NCH):
            got(out.at[chunk_rows(c)], OUT, c)

    for j in range(2):
        for p in range(PIECES):
            z_piece(j, p).wait_send()
            far_two(j, p).wait_send()
            for s in range(2):
                far_x(j, p, s).wait_send()
            for i in range(4):
                far_sib(j, p, i).wait_send()
        for s in range(2):
            copy(stale[j], block(bufs[j], 2), KV_NEAR, 2 * j + s, at_x(1)).wait_send()
        for i in range(4):
            near_sib(j, i).wait_send()
        near_two(j).wait_send()

    for m in (1, 2):
        @pl.when(t != m)
        def _(m=m):
            for c in range(NCH):
                img_copy(m, c).wait_send()
                tail_copy(m, c).wait_send()

    @pl.when(is_mid)
    def _():
        for d in (1, 2, 3):
            w_b(d).wait_send()
            o_b(d).wait_send()
            o_c(d).wait_send()
        for j in range(3):
            w_d(j).wait_send()
            for s in (0, 1):
                w_c(j, s).wait_send()
                w_two(j, s).wait_send()
        o_d().wait_send()
        for c in range(NCH):
            out_copy(c).wait_send()
            for j in range(3):
                qkv_copy(j, c).wait_send()


def shards(image, modulation, w_query, w_key, w_value, w_out, query_gain, key_gain, text_keys, text_values, stale_keys, stale_values):
    hbm = pl.BlockSpec(memory_space=pl.ANY)
    vmem = pl.BlockSpec(memory_space=pltpu.VMEM)
    return pl.pallas_call(
        kernel,
        out_shape=jax.ShapeDtypeStruct((ROWS, SLICE), BF),
        in_specs=[hbm, vmem, hbm, hbm, hbm, hbm, vmem, vmem, hbm, hbm, hbm, hbm],
        out_specs=vmem,
        scratch_shapes=[
            pltpu.VMEM((17 * ROWS, WIDE), BF),
            pltpu.VMEM((17 * ROWS, WIDE), BF),
            pltpu.VMEM((4, ROWS, SLICE), BF),
            pltpu.VMEM((3, DM, WIDE), BF),
            pltpu.VMEM((3, DM, WIDE), BF),
            pltpu.VMEM((4, WIDE, 2 * SLICE), BF),
            pltpu.VMEM((CH, DM), BF),
            pltpu.VMEM((ROWS, WIDE), BF),
            pltpu.VMEM((3, ROWS, WIDE), BF),
            pltpu.VMEM((4, ROWS, WIDE), BF),
            pltpu.VMEM((ROWS, SLICE), BF),
            pltpu.VMEM((HEADS, ROWS, HW), F32),
            pltpu.VMEM((HEADS, ROWS, 2 * HW), F32),
            pltpu.SemaphoreType.DMA((NSEM,)),
            pltpu.SemaphoreType.DMA((NSEM,)),
            pltpu.SemaphoreType.DMA((8,)),
        ],
        compiler_params=pltpu.CompilerParams(
            collective_id=0, has_side_effects=True, vmem_limit_bytes=60 * 1024 * 1024
        ),
        cost_estimate=pl.CostEstimate(
            flops=12_000_000_000, bytes_accessed=20_000_000, transcendentals=14_000_000
        ),
        name="joint_attention",
    )(
        image, modulation, w_query, w_key, w_value, w_out,
        query_gain.reshape(1, HW), key_gain.reshape(1, HW),
        text_keys, text_values, stale_keys, stale_values,
    )


def solution(mesh):
    rows = P(("batch", "patch"), "tensor")
    cols = P(None, "tensor")
    in_specs = (
        rows, P("batch", None), cols, cols, cols, P("tensor", None), P(), P(),
        P("batch", "tensor"), P("batch", "tensor"), rows, rows,
    )
    return jax.shard_map(shards, mesh=mesh, in_specs=in_specs, out_specs=rows, check_vma=False)
```

```python
import functools
import math

import jax
import jax.numpy as jnp
from jax import lax
from jax.experimental import pallas as pl
from jax.experimental.pallas import tpu as pltpu
from jax.sharding import PartitionSpec as P

MESH = pl.DeviceIdType.MESH
BF = jnp.bfloat16
F32 = jnp.float32
ROWS = 512
HW = 128
HEADS = 3
WIDE = HEADS * HW
SLICE = 768
DM = 4 * SLICE
CH = 128
NCH = ROWS // CH
KB = 2048
PIECES = 2
LOG2E = 1.4426950408889634

KV_NEAR = 0
KV_TWO = KV_NEAR + 4
KV_SIB = KV_TWO + 2
KV_Z = KV_SIB + 8
KV_FX = KV_Z + 2 * PIECES
KV_FTWO = KV_FX + 4 * PIECES
KV_FSIB = KV_FTWO + 2 * PIECES
W_A = KV_FSIB + 8 * PIECES
W_B = W_A + 3
W_C = W_B + 9
W_D = W_C + 12
O_A = W_D + 3
O_B = O_A + 4
O_C = O_B + 3
O_D = O_C + 3
IMG = O_D + 1
QKV = IMG + 4 * NCH
TAIL = QKV + 3 * NCH
OUT = TAIL + 4 * NCH
NSEM = OUT + NCH


def kernel(
    img_h, mod, wq_h, wk_h, wv_h, wo_h, qgain, kgain, tk_h, tv_h, sk_h, sv_h,
    out,
    kbuf, vbuf, img, w_own, w_end, w_o, modl, qbuf, stage, att, ostage, m_s, acc_s,
    ssem, rsem, lsem,
):
    yy = lax.axis_index("batch")
    patch = lax.axis_index("patch")
    t = lax.axis_index("tensor")
    zh = patch // 8
    xx = lax.rem(patch, 8) // 2
    cc = lax.rem(patch, 2)
    is_mid = (t == 1) | (t == 2)
    is_end = (t == 0) | (t == 3)
    pair = jnp.where(t < 2, 1 - t, 5 - t)

    def at_x(d):
        return {"patch": zh * 8 + lax.rem(xx + d + 4, 4) * 2 + cc}

    def at_y(d):
        return {"batch": lax.rem(yy + d + 4, 4)}

    sib = {"patch": zh * 8 + xx * 2 + (1 - cc)}
    far = {"patch": (1 - zh) * 8 + xx * 2 + cc}
    to_pair = {"tensor": pair}

    def copy(src, dst, base, off, dev):
        i = base + off
        return pltpu.make_async_remote_copy(
            src_ref=src, dst_ref=dst, send_sem=ssem.at[i], recv_sem=rsem.at[i],
            device_id=dev, device_id_type=MESH,
        )

    def got(dst, base, off=0):
        copy(dst, dst, base, off, sib).wait_recv()

    def block(buf, slot, piece=0, pieces=1):
        n = ROWS // pieces
        return buf.at[pl.ds(slot * ROWS + piece * n, n)]

    local = [
        pltpu.make_async_copy(wq_h, w_own.at[0], lsem.at[0]),
        pltpu.make_async_copy(wk_h, w_own.at[1], lsem.at[1]),
        pltpu.make_async_copy(wv_h, w_own.at[2], lsem.at[2]),
        pltpu.make_async_copy(tk_h, block(kbuf, 0), lsem.at[3]),
        pltpu.make_async_copy(tv_h, block(vbuf, 0), lsem.at[4]),
        pltpu.make_async_copy(img_h, img.at[t], lsem.at[5]),
    ]
    my_cols = pl.ds(pl.multiple_of(t * SLICE, SLICE), SLICE)
    pair_cols = pl.ds(pl.multiple_of(pair * SLICE, SLICE), SLICE)
    local_o = [
        pltpu.make_async_copy(wo_h.at[:, my_cols], w_o.at[0, :, pl.ds(0, SLICE)], lsem.at[6]),
        pltpu.make_async_copy(wo_h.at[:, pair_cols], w_o.at[0, :, pl.ds(SLICE, SLICE)], lsem.at[7]),
    ]

    for cp in local:
        cp.start()

    @pl.when(is_mid)
    def _():
        for cp in local_o:
            cp.start()

    peers = [sib, far] + [at_x(d) for d in (1, 2, 3)] + [at_y(d) for d in (1, 2, 3)]
    peers += [{"tensor": lax.rem(t + d, 4)} for d in (1, 2, 3)]
    barrier = pltpu.get_barrier_semaphore()
    for p in peers:
        pl.semaphore_signal(barrier, inc=1, device_id=p, device_id_type=MESH)
    pl.semaphore_wait(barrier, len(peers))

    stale = (sk_h, sv_h)
    bufs = (kbuf, vbuf)

    def z_piece(j, p):
        n = ROWS // PIECES
        return copy(
            stale[j].at[pl.ds(p * n, n)], block(bufs[j], 8, p, PIECES), KV_Z, j * PIECES + p, far
        )

    w_rows = pl.ds(pl.multiple_of(cc * 1536 + yy * 384 + xx * 96, 96), 96)

    def w_a(j):
        return copy((wq_h, wk_h, wv_h)[j].at[w_rows], w_end.at[j, w_rows], W_A, j, to_pair)

    @pl.when(is_end)
    def _():
        for j in range(3):
            w_a(j).start()

    def img_copy(m, c):
        r = lax.rem(t - m + 4, 4)
        rows = pl.ds(pl.multiple_of(c * CH, CH), CH)
        return copy(img_h.at[rows], img.at[t, rows], IMG, r * NCH + c, {"tensor": jnp.int32(m)})

    def start_img(c):
        for m in (1, 2):
            @pl.when(t != m)
            def _(m=m):
                img_copy(m, c).start()

    o_rows = pl.ds(pl.multiple_of(cc * 192 + yy * 48, 48), 48)
    o_cols = pl.ds(pl.multiple_of(xx * 384, 384), 384)

    def o_a(m):
        r = lax.rem(t - m + 4, 4)
        e = 3 * (m - 1)
        start = jnp.where(xx < 2, m, e) * SLICE + lax.rem(xx, 2) * 384
        src = wo_h.at[o_rows, pl.ds(pl.multiple_of(start, 384), 384)]
        return copy(src, w_o.at[r, o_rows, o_cols], O_A, r, {"tensor": jnp.int32(m)})

    for m in (1, 2):
        @pl.when(t != m)
        def _(m=m):
            o_a(m).start()

    m_s[...] = jnp.full(m_s.shape, -1e30, F32)
    acc_s[...] = jnp.zeros(acc_s.shape, F32)

    def w_b(j, d):
        piece = w_end.at[j, w_rows]
        return copy(piece, piece, W_B, 3 * j + d - 1, at_x(d))

    def y_rows(d, half=None):
        n = 384 if half is None else 192
        first = cc * 1536 + lax.rem(yy + d + 4, 4) * 384 + (192 if half else 0)
        return pl.ds(pl.multiple_of(first, n), n)

    def w_c(j, s):
        piece = w_end.at[j, y_rows(0)]
        return copy(piece, piece, W_C, 2 * j + s, at_y(1 - 2 * s))

    def w_two(j, s):
        piece = w_end.at[j, y_rows(2 * s - 1, s)]
        return copy(piece, piece, W_C, 6 + 2 * j + s, at_y(1 - 2 * s))

    def w_d(j):
        piece = w_end.at[j, pl.ds(pl.multiple_of(cc * 1536, 1536), 1536)]
        return copy(piece, piece, W_D, j, sib)

    def w_forward(j):
        for s in (0, 1):
            got(w_end.at[j, y_rows(2 * s - 1)], W_C, 2 * j + s)
            w_two(j, s).start()

    def w_share(j):
        for s in (0, 1):
            got(w_end.at[j, y_rows(2, s)], W_C, 6 + 2 * j + s)
        w_d(j).start()

    def o_b(d):
        piece = w_o.at[pl.ds(1, 3), o_rows, o_cols]
        return copy(piece, piece, O_B, d - 1, at_x(d))

    def o_c(d):
        piece = w_o.at[pl.ds(1, 3), o_rows]
        return copy(piece, piece, O_C, d - 1, at_y(d))

    def o_d():
        piece = w_o.at[pl.ds(1, 3), pl.ds(pl.multiple_of(cc * 192, 192), 192)]
        return copy(piece, piece, O_D, 0, sib)

    def wait_w_b(j):
        for d in (1, 2, 3):
            rows = pl.ds(pl.multiple_of(cc * 1536 + yy * 384 + lax.rem(xx - d + 4, 4) * 96, 96), 96)
            got(w_end.at[j, rows], W_B, 3 * j + d - 1)

    def wait_o_b():
        for d in (1, 2, 3):
            cols = pl.ds(pl.multiple_of(lax.rem(xx - d + 4, 4) * 384, 384), 384)
            got(w_o.at[pl.ds(1, 3), o_rows, cols], O_B, d - 1)

    def wait_o_c():
        for d in (1, 2, 3):
            rows = pl.ds(pl.multiple_of(cc * 192 + lax.rem(yy - d + 4, 4) * 48, 48), 48)
            got(w_o.at[pl.ds(1, 3), rows], O_C, d - 1)

    def near_sib(j, i):
        src = stale[j] if i == 0 else block(bufs[j], 2 * i)
        return copy(src, block(bufs[j], 2 * i + 1), KV_SIB, 4 * j + i, sib)

    def near_two(j):
        if j == 0:
            return copy(block(kbuf, 4), block(kbuf, 6), KV_TWO, 0, at_x(1))
        return copy(block(vbuf, 2), block(vbuf, 6), KV_TWO, 1, at_x(-1))

    def far_x(j, p, s):
        src = block(bufs[j], 8, p, PIECES)
        dst = block(bufs[j], 10 + 2 * s, p, PIECES)
        return copy(src, dst, KV_FX, (j * PIECES + p) * 2 + s, at_x(-1 if s == 0 else 1))

    def far_two(j, p):
        src = block(bufs[j], 12 if j == 0 else 10, p, PIECES)
        dst = block(bufs[j], 14, p, PIECES)
        return copy(src, dst, KV_FTWO, j * PIECES + p, at_x(1 if j == 0 else -1))

    def far_sib(j, p, i):
        src = block(bufs[j], 8 + 2 * i, p, PIECES)
        dst = block(bufs[j], 9 + 2 * i, p, PIECES)
        return copy(src, dst, KV_FSIB, (j * PIECES + p) * 4 + i, sib)

    def far_z(j, p):
        got(block(bufs[j], 8, p, PIECES), KV_Z, j * PIECES + p)
        far_x(j, p, 0).start()
        far_x(j, p, 1).start()
        far_sib(j, p, 0).start()

    def far_on(p):
        for j in range(2):
            for s in (0, 1):
                got(block(bufs[j], 10 + 2 * s, p, PIECES), KV_FX, (j * PIECES + p) * 2 + s)
            far_two(j, p).start()
            far_sib(j, p, 1).start()
            far_sib(j, p, 2).start()

    def far_last():
        for p in range(PIECES):
            for j in range(2):
                got(block(bufs[j], 14, p, PIECES), KV_FTWO, j * PIECES + p)
                far_sib(j, p, 3).start()

    def far_rest():
        for p in range(PIECES):
            for j in range(2):
                for i in range(4):
                    got(
                        block(bufs[j], 9 + 2 * i, p, PIECES),
                        KV_FSIB, (j * PIECES + p) * 4 + i,
                    )

    def near_on():
        got(block(kbuf, 4), KV_NEAR, 1)
        near_two(0).start()
        got(block(vbuf, 2), KV_NEAR, 2)
        near_two(1).start()
        near_sib(0, 2).start()
        near_sib(1, 1).start()
        got(block(kbuf, 2), KV_NEAR)
        near_sib(0, 1).start()
        got(block(vbuf, 4), KV_NEAR, 3)
        near_sib(1, 2).start()

    def near_last():
        for j in range(2):
            got(block(bufs[j], 6), KV_TWO, j)
            near_sib(j, 3).start()

    def start_near():
        for j in range(2):
            copy(stale[j], block(bufs[j], 2), KV_NEAR, 2 * j, at_x(-1)).start()
            copy(stale[j], block(bufs[j], 4), KV_NEAR, 2 * j + 1, at_x(1)).start()

    for j in range(2):
        copy(stale[j], block(bufs[j], 1), KV_SIB, 4 * j, sib).start()

    @pl.when(is_end)
    def _():
        start_near()
        for j in range(3):
            w_a(j).wait_send()

    @pl.when(is_mid)
    def _():
        for j in range(3):
            got(w_end.at[j, w_rows], W_A, j)
            for d in (1, 2, 3):
                w_b(j, d).start()

    for m in (1, 2):
        @pl.when(t != m)
        def _(m=m):
            o_a(m).wait_send()

    @pl.when(is_mid)
    def _():
        for r in (1, 2, 3):
            got(w_o.at[r, o_rows, o_cols], O_A, r)

    for p in range(PIECES):
        for j in range(2):
            z_piece(j, p).start()

    for c in range(NCH):
        start_img(c)

    def chunk_rows(c, base=0):
        return pl.ds(pl.multiple_of(base + c * CH, CH), CH)

    def norm_chunk(c):
        rows = chunk_rows(c)
        total = jnp.zeros((CH, 1), F32)
        for s in range(4):
            total += jnp.sum(img[s, rows].astype(F32), axis=1, keepdims=True)
        mean = total * (1.0 / DM)
        total = jnp.zeros((CH, 1), F32)
        for s in range(4):
            d = img[s, rows].astype(F32) - mean
            total += jnp.sum(d * d, axis=1, keepdims=True)
        rstd = lax.rsqrt(total * (1.0 / DM) + 1e-06)
        for s in range(4):
            cols = slice(s * SLICE, (s + 1) * SLICE)
            d = (img[s, rows].astype(F32) - mean) * rstd
            modl[rows, cols] = (d * (1.0 + mod[1:2, cols]) + mod[0:1, cols]).astype(BF)

    def project(c, w, put):
        for j in (1, 2, 0):
            y = jnp.dot(modl[chunk_rows(c)], w[j], preferred_element_type=F32)
            if j == 2:
                put(c, j, y.astype(BF))
                continue
            gain = qgain[...] * (LOG2E / math.sqrt(HW)) if j == 0 else kgain[...]
            parts = []
            for h in range(HEADS):
                v = y[:, h * HW : (h + 1) * HW]
                power = jnp.mean(v * v, axis=1, keepdims=True)
                parts.append((v * lax.rsqrt(power + 1e-06) * gain).astype(BF))
            put(c, j, jnp.concatenate(parts, axis=1))

    FRESH = 16 * ROWS

    def qkv_copy(j, c):
        dst = (
            qbuf.at[chunk_rows(c)],
            kbuf.at[chunk_rows(c, FRESH)],
            vbuf.at[chunk_rows(c, FRESH)],
        )[j]
        return copy(stage.at[j, chunk_rows(c)], dst, QKV, j * NCH + c, to_pair)

    def image_chunk(c):
        for r in (1, 2, 3):
            s = lax.rem(t + r, 4)
            got(img.at[s, chunk_rows(c)], IMG, r * NCH + c)
        norm_chunk(c)

    def put_end(c, j, v):
        stage[j, chunk_rows(c)] = v
        qkv_copy(j, c).start()

    def put_own(c, j, v):
        if j == 0:
            qbuf[chunk_rows(c)] = v
        else:
            bufs[j - 1][chunk_rows(c, FRESH)] = v

    def middle_chunk(c):
        @pl.when(c > 0)
        def _():
            image_chunk(c)

        project(c, w_end, put_end)

        @pl.when(c > 0)
        def _():
            project(c, w_own, put_own)

    def end_fresh(c):
        got(kbuf.at[chunk_rows(c, FRESH)], QKV, NCH + c)
        got(vbuf.at[chunk_rows(c, FRESH)], QKV, 2 * NCH + c)

    def end_query(c):
        got(qbuf.at[chunk_rows(c)], QKV, c)

    def fresh_chunk(c):
        @pl.when(is_mid)
        def _():
            middle_chunk(c)

        @pl.when(is_end)
        def _():
            end_fresh(c)
            end_query(c)

    for cp in local:
        cp.wait()

    @pl.when(is_end)
    def _():
        far_z(0, 0)
        far_z(1, 0)
        near_on()
        far_z(0, 1)
        far_z(1, 1)
        far_on(0)
        near_last()
        far_on(1)
        far_last()

    @pl.when(is_mid)
    def _():
        for j in range(3):
            wait_w_b(j)
            for s in (0, 1):
                w_c(j, s).start()
        start_near()
        for d in (1, 2, 3):
            o_b(d).start()
        w_forward(0)
        w_forward(1)
        far_z(0, 0)
        far_z(1, 0)
        w_forward(2)
        near_on()
        w_share(0)
        far_z(0, 1)
        w_share(1)
        far_z(1, 1)
        w_share(2)
        wait_o_b()
        for d in (1, 2, 3):
            o_c(d).start()
        far_on(0)
        near_last()
        image_chunk(0)
        project(0, w_own, put_own)

    def near_rest():
        for j in range(2):
            for i in range(4):
                got(block(bufs[j], 2 * i + 1), KV_SIB, 4 * j + i)

    def attend(c, start, n):
        rows = chunk_rows(c)
        keys = pl.ds(pl.multiple_of(start, ROWS), n)
        for h in range(HEADS):
            cols = slice(h * HW, (h + 1) * HW)
            k = kbuf[keys, cols]
            v = vbuf[keys, cols]
            s = lax.dot_general(
                qbuf[rows, cols], k, (((1,), (1,)), ((), ())), preferred_element_type=F32
            )
            old = m_s[h, rows]
            new = jnp.maximum(old, jnp.max(s, axis=1, keepdims=True))
            shrink = jnp.exp2(old - new)
            p = jnp.exp2(s - new[:, :1]).astype(BF)
            m_s[h, rows] = new
            both = jnp.concatenate([v, jnp.ones_like(v)], axis=1)
            pv = jnp.dot(p, both, preferred_element_type=F32)
            acc_s[h, rows] = acc_s[h, rows] * jnp.concatenate([shrink, shrink], axis=1) + pv

    other = jnp.where(is_mid, 3 - t, pair)
    from_end = lax.rem(pair - t + 4, 4)

    def tail_copy(c):
        rows = chunk_rows(c)
        r = lax.rem(t - other + 4, 4)
        return copy(att.at[0, rows], att.at[r, rows], TAIL, r * NCH + c, {"tensor": other})

    def relay_copy(c):
        rows = chunk_rows(c)
        src = att.at[from_end, rows]
        return copy(src, att.at[2, rows], TAIL, 2 * NCH + c, {"tensor": other})

    def relay(c):
        got(att.at[from_end, chunk_rows(c)], TAIL, from_end * NCH + c)
        relay_copy(c).start()

    def finish(c):
        attend(c, FRESH, ROWS)
        rows = chunk_rows(c)
        for h in range(HEADS):
            a = acc_s[h, rows]
            att[0, rows, h * HW : (h + 1) * HW] = (a[:, :HW] / a[:, HW:]).astype(BF)
        tail_copy(c).start()

    def out_copy(c):
        return copy(ostage.at[chunk_rows(c)], out.at[chunk_rows(c)], OUT, c, to_pair)

    def project_out(c):
        rows = chunk_rows(c)
        r = 4 - from_end
        got(att.at[r, rows], TAIL, r * NCH + c)
        got(att.at[2, rows], TAIL, 2 * NCH + c)
        for half, cols in ((1, pair_cols), (0, my_cols)):
            y = jnp.zeros((CH, SLICE), F32)
            for r in range(4):
                w = w_o[r, :, half * SLICE : (half + 1) * SLICE]
                y += jnp.dot(att[r, rows], w, preferred_element_type=F32)
            y = (y * mod[2:3, cols]).astype(BF)
            if half:
                ostage[rows] = y
                out_copy(c).start()
            else:
                out[rows] = y

    @pl.when(is_mid)
    def _():
        for cp in local_o:
            cp.wait()
        for j in range(3):
            rows = pl.ds(pl.multiple_of((1 - cc) * 1536, 1536), 1536)
            got(w_end.at[j, rows], W_D, j)

    def near(c):
        @pl.loop(0, 4096 // KB)
        def _(b):
            attend(c, b * KB, KB)

    def distant(c):
        @pl.loop(4096 // KB, 8192 // KB)
        def _(b):
            attend(c, b * KB, KB)

    @pl.loop(0, NCH - 1)
    def _(c):
        fresh_chunk(c)

        @pl.when(c == 0)
        def _():
            near_rest()

        near(c)

        @pl.when((c == 0) & is_mid)
        def _():
            far_on(1)

        @pl.when(c == 1)
        def _():
            @pl.when(is_mid)
            def _():
                far_last()

            far_rest()

        @pl.when(c > 0)
        def _():
            distant(c - 1)

    @pl.when(is_mid)
    def _():
        wait_o_c()
        o_d().start()
        middle_chunk(NCH - 1)

    distant(NCH - 2)

    @pl.when(is_end)
    def _():
        end_fresh(NCH - 1)

    @pl.loop(0, NCH - 1)
    def _(c):
        finish(c)

    @pl.when(is_end)
    def _():
        end_query(NCH - 1)

    @pl.loop(0, 8192 // KB)
    def _(b):
        attend(NCH - 1, b * KB, KB)

        @pl.when((b > 0) & is_mid)
        def _():
            relay(b - 1)

            @pl.when(b == 8192 // KB - 1)
            def _():
                got(w_o.at[pl.ds(1, 3), pl.ds(pl.multiple_of((1 - cc) * 192, 192), 192)], O_D)
                project_out(0)

    finish(NCH - 1)

    @pl.when(is_mid)
    def _():
        @pl.loop(1, NCH)
        def _(c):
            @pl.when(c == 2)
            def _():
                relay(NCH - 1)

            project_out(c)

    @pl.when(is_end)
    def _():
        for c in range(NCH):
            got(out.at[chunk_rows(c)], OUT, c)

    for j in range(2):
        for p in range(PIECES):
            z_piece(j, p).wait_send()
            far_two(j, p).wait_send()
            for s in range(2):
                far_x(j, p, s).wait_send()
            for i in range(4):
                far_sib(j, p, i).wait_send()
        for s in range(2):
            copy(stale[j], block(bufs[j], 2), KV_NEAR, 2 * j + s, at_x(1)).wait_send()
        for i in range(4):
            near_sib(j, i).wait_send()
        near_two(j).wait_send()

    for m in (1, 2):
        @pl.when(t != m)
        def _(m=m):
            for c in range(NCH):
                img_copy(m, c).wait_send()

    for c in range(NCH):
        tail_copy(c).wait_send()

    @pl.when(is_mid)
    def _():
        for d in (1, 2, 3):
            for j in range(3):
                w_b(j, d).wait_send()
            o_b(d).wait_send()
            o_c(d).wait_send()
        for j in range(3):
            w_d(j).wait_send()
            for s in (0, 1):
                w_c(j, s).wait_send()
                w_two(j, s).wait_send()
        o_d().wait_send()
        for c in range(NCH):
            out_copy(c).wait_send()
            relay_copy(c).wait_send()
            for j in range(3):
                qkv_copy(j, c).wait_send()


def shards(image, modulation, w_query, w_key, w_value, w_out, query_gain, key_gain, text_keys, text_values, stale_keys, stale_values):
    hbm = pl.BlockSpec(memory_space=pl.ANY)
    vmem = pl.BlockSpec(memory_space=pltpu.VMEM)
    return pl.pallas_call(
        kernel,
        out_shape=jax.ShapeDtypeStruct((ROWS, SLICE), BF),
        in_specs=[hbm, vmem, hbm, hbm, hbm, hbm, vmem, vmem, hbm, hbm, hbm, hbm],
        out_specs=vmem,
        scratch_shapes=[
            pltpu.VMEM((17 * ROWS, WIDE), BF),
            pltpu.VMEM((17 * ROWS, WIDE), BF),
            pltpu.VMEM((4, ROWS, SLICE), BF),
            pltpu.VMEM((3, DM, WIDE), BF),
            pltpu.VMEM((3, DM, WIDE), BF),
            pltpu.VMEM((4, WIDE, 2 * SLICE), BF),
            pltpu.VMEM((ROWS, DM), BF),
            pltpu.VMEM((ROWS, WIDE), BF),
            pltpu.VMEM((3, ROWS, WIDE), BF),
            pltpu.VMEM((4, ROWS, WIDE), BF),
            pltpu.VMEM((ROWS, SLICE), BF),
            pltpu.VMEM((HEADS, ROWS, HW), F32),
            pltpu.VMEM((HEADS, ROWS, 2 * HW), F32),
            pltpu.SemaphoreType.DMA((NSEM,)),
            pltpu.SemaphoreType.DMA((NSEM,)),
            pltpu.SemaphoreType.DMA((8,)),
        ],
        compiler_params=pltpu.CompilerParams(
            collective_id=0, has_side_effects=True, vmem_limit_bytes=60 * 1024 * 1024
        ),
        cost_estimate=pl.CostEstimate(
            flops=12_000_000_000, bytes_accessed=20_000_000, transcendentals=14_000_000
        ),
        name="joint_attention",
    )(
        image, modulation, w_query, w_key, w_value, w_out,
        query_gain.reshape(1, HW), key_gain.reshape(1, HW),
        text_keys, text_values, stale_keys, stale_values,
    )


def solution(mesh):
    rows = P(("batch", "patch"), "tensor")
    cols = P(None, "tensor")
    in_specs = (
        rows, P("batch", None), cols, cols, cols, P("tensor", None), P(), P(),
        P("batch", "tensor"), P("batch", "tensor"), rows, rows,
    )
    return jax.shard_map(shards, mesh=mesh, in_specs=in_specs, out_specs=rows, check_vma=False)
```

```python
import functools
import math

import jax
import jax.numpy as jnp
from jax import lax
from jax.experimental import pallas as pl
from jax.experimental.pallas import tpu as pltpu
from jax.sharding import PartitionSpec as P

MESH = pl.DeviceIdType.MESH
BF = jnp.bfloat16
F32 = jnp.float32
ROWS = 512
HW = 128
HEADS = 3
WIDE = HEADS * HW
SLICE = 768
DM = 4 * SLICE
CH = 128
NCH = ROWS // CH
KB = 2048
PIECES = 2
LOG2E = 1.4426950408889634

KV_NEAR = 0
KV_TWO = KV_NEAR + 4
KV_SIB = KV_TWO + 2
KV_Z = KV_SIB + 8
KV_FX = KV_Z + 2 * PIECES
KV_FTWO = KV_FX + 4 * PIECES
KV_FSIB = KV_FTWO + 2 * PIECES
W_A = KV_FSIB + 8 * PIECES
W_B = W_A + 3
W_C = W_B + 9
W_D = W_C + 12
O_A = W_D + 3
O_B = O_A + 4
O_C = O_B + 3
O_D = O_C + 3
IMG = O_D + 1
QKV = IMG + 4 * NCH
TAIL = QKV + 3 * NCH
OUT = TAIL + 4 * NCH
NSEM = OUT + NCH


def kernel(
    img_h, mod, wq_h, wk_h, wv_h, wo_h, qgain, kgain, tk_h, tv_h, sk_h, sv_h,
    out,
    kbuf, vbuf, img, w_own, w_end, w_o, modl, qbuf, stage, att, ostage, m_s, acc_s,
    ssem, rsem, lsem,
):
    yy = lax.axis_index("batch")
    patch = lax.axis_index("patch")
    t = lax.axis_index("tensor")
    zh = patch // 8
    xx = lax.rem(patch, 8) // 2
    cc = lax.rem(patch, 2)
    is_mid = (t == 1) | (t == 2)
    is_end = (t == 0) | (t == 3)
    pair = jnp.where(t < 2, 1 - t, 5 - t)

    def at_x(d):
        return {"patch": zh * 8 + lax.rem(xx + d + 4, 4) * 2 + cc}

    def at_y(d):
        return {"batch": lax.rem(yy + d + 4, 4)}

    sib = {"patch": zh * 8 + xx * 2 + (1 - cc)}
    far = {"patch": (1 - zh) * 8 + xx * 2 + cc}
    to_pair = {"tensor": pair}

    def copy(src, dst, base, off, dev):
        i = base + off
        return pltpu.make_async_remote_copy(
            src_ref=src, dst_ref=dst, send_sem=ssem.at[i], recv_sem=rsem.at[i],
            device_id=dev, device_id_type=MESH,
        )

    def got(dst, base, off=0):
        copy(dst, dst, base, off, sib).wait_recv()

    def block(buf, slot, piece=0, pieces=1):
        n = ROWS // pieces
        return buf.at[pl.ds(slot * ROWS + piece * n, n)]

    local = [
        pltpu.make_async_copy(wq_h, w_own.at[0], lsem.at[0]),
        pltpu.make_async_copy(wk_h, w_own.at[1], lsem.at[1]),
        pltpu.make_async_copy(wv_h, w_own.at[2], lsem.at[2]),
        pltpu.make_async_copy(tk_h, block(kbuf, 0), lsem.at[3]),
        pltpu.make_async_copy(tv_h, block(vbuf, 0), lsem.at[4]),
        pltpu.make_async_copy(img_h, img.at[t], lsem.at[5]),
    ]
    my_cols = pl.ds(pl.multiple_of(t * SLICE, SLICE), SLICE)
    pair_cols = pl.ds(pl.multiple_of(pair * SLICE, SLICE), SLICE)
    local_o = [
        pltpu.make_async_copy(wo_h.at[:, my_cols], w_o.at[0, :, pl.ds(0, SLICE)], lsem.at[6]),
        pltpu.make_async_copy(wo_h.at[:, pair_cols], w_o.at[0, :, pl.ds(SLICE, SLICE)], lsem.at[7]),
    ]

    for cp in local:
        cp.start()

    @pl.when(is_mid)
    def _():
        for cp in local_o:
            cp.start()

    peers = [sib, far] + [at_x(d) for d in (1, 2, 3)] + [at_y(d) for d in (1, 2, 3)]
    peers += [{"tensor": lax.rem(t + d, 4)} for d in (1, 2, 3)]
    barrier = pltpu.get_barrier_semaphore()
    for p in peers:
        pl.semaphore_signal(barrier, inc=1, device_id=p, device_id_type=MESH)
    pl.semaphore_wait(barrier, len(peers))

    stale = (sk_h, sv_h)
    bufs = (kbuf, vbuf)

    def z_piece(j, p):
        n = ROWS // PIECES
        return copy(
            stale[j].at[pl.ds(p * n, n)], block(bufs[j], 8, p, PIECES), KV_Z, j * PIECES + p, far
        )

    w_rows = pl.ds(pl.multiple_of(cc * 1536 + yy * 384 + xx * 96, 96), 96)

    def w_a(j):
        return copy((wq_h, wk_h, wv_h)[j].at[w_rows], w_end.at[j, w_rows], W_A, j, to_pair)

    @pl.when(is_end)
    def _():
        for j in range(3):
            w_a(j).start()

    def img_copy(m, c):
        r = lax.rem(t - m + 4, 4)
        rows = pl.ds(pl.multiple_of(c * CH, CH), CH)
        return copy(img_h.at[rows], img.at[t, rows], IMG, r * NCH + c, {"tensor": jnp.int32(m)})

    def start_img(c):
        for m in (1, 2):
            @pl.when(t != m)
            def _(m=m):
                img_copy(m, c).start()

    o_rows = pl.ds(pl.multiple_of(cc * 192 + yy * 48, 48), 48)
    o_cols = pl.ds(pl.multiple_of(xx * 384, 384), 384)

    def o_a(m):
        r = lax.rem(t - m + 4, 4)
        e = 3 * (m - 1)
        start = jnp.where(xx < 2, m, e) * SLICE + lax.rem(xx, 2) * 384
        src = wo_h.at[o_rows, pl.ds(pl.multiple_of(start, 384), 384)]
        return copy(src, w_o.at[r, o_rows, o_cols], O_A, r, {"tensor": jnp.int32(m)})

    for m in (1, 2):
        @pl.when(t != m)
        def _(m=m):
            o_a(m).start()

    m_s[...] = jnp.full(m_s.shape, -1e30, F32)
    acc_s[...] = jnp.zeros(acc_s.shape, F32)

    def w_b(j, d):
        piece = w_end.at[j, w_rows]
        return copy(piece, piece, W_B, 3 * j + d - 1, at_x(d))

    def y_rows(d, half=None):
        n = 384 if half is None else 192
        first = cc * 1536 + lax.rem(yy + d + 4, 4) * 384 + (192 if half else 0)
        return pl.ds(pl.multiple_of(first, n), n)

    def w_c(j, s):
        piece = w_end.at[j, y_rows(0)]
        return copy(piece, piece, W_C, 2 * j + s, at_y(1 - 2 * s))

    def w_two(j, s):
        piece = w_end.at[j, y_rows(2 * s - 1, s)]
        return copy(piece, piece, W_C, 6 + 2 * j + s, at_y(1 - 2 * s))

    def w_d(j):
        piece = w_end.at[j, pl.ds(pl.multiple_of(cc * 1536, 1536), 1536)]
        return copy(piece, piece, W_D, j, sib)

    def w_forward(j):
        for s in (0, 1):
            got(w_end.at[j, y_rows(2 * s - 1)], W_C, 2 * j + s)
            w_two(j, s).start()

    def w_share(j):
        for s in (0, 1):
            got(w_end.at[j, y_rows(2, s)], W_C, 6 + 2 * j + s)
        w_d(j).start()

    def o_b(d):
        piece = w_o.at[pl.ds(1, 3), o_rows, o_cols]
        return copy(piece, piece, O_B, d - 1, at_x(d))

    def o_c(d):
        piece = w_o.at[pl.ds(1, 3), o_rows]
        return copy(piece, piece, O_C, d - 1, at_y(d))

    def o_d():
        piece = w_o.at[pl.ds(1, 3), pl.ds(pl.multiple_of(cc * 192, 192), 192)]
        return copy(piece, piece, O_D, 0, sib)

    def wait_w_b(j):
        for d in (1, 2, 3):
            rows = pl.ds(pl.multiple_of(cc * 1536 + yy * 384 + lax.rem(xx - d + 4, 4) * 96, 96), 96)
            got(w_end.at[j, rows], W_B, 3 * j + d - 1)

    def wait_o_b():
        for d in (1, 2, 3):
            cols = pl.ds(pl.multiple_of(lax.rem(xx - d + 4, 4) * 384, 384), 384)
            got(w_o.at[pl.ds(1, 3), o_rows, cols], O_B, d - 1)

    def wait_o_c():
        for d in (1, 2, 3):
            rows = pl.ds(pl.multiple_of(cc * 192 + lax.rem(yy - d + 4, 4) * 48, 48), 48)
            got(w_o.at[pl.ds(1, 3), rows], O_C, d - 1)

    def near_sib(j, i):
        src = stale[j] if i == 0 else block(bufs[j], 2 * i)
        return copy(src, block(bufs[j], 2 * i + 1), KV_SIB, 4 * j + i, sib)

    def near_two(j):
        if j == 0:
            return copy(block(kbuf, 4), block(kbuf, 6), KV_TWO, 0, at_x(1))
        return copy(block(vbuf, 2), block(vbuf, 6), KV_TWO, 1, at_x(-1))

    def far_x(j, p, s):
        src = block(bufs[j], 8, p, PIECES)
        dst = block(bufs[j], 10 + 2 * s, p, PIECES)
        return copy(src, dst, KV_FX, (j * PIECES + p) * 2 + s, at_x(-1 if s == 0 else 1))

    def far_two(j, p):
        src = block(bufs[j], 12 if j == 0 else 10, p, PIECES)
        dst = block(bufs[j], 14, p, PIECES)
        return copy(src, dst, KV_FTWO, j * PIECES + p, at_x(1 if j == 0 else -1))

    def far_sib(j, p, i):
        src = block(bufs[j], 8 + 2 * i, p, PIECES)
        dst = block(bufs[j], 9 + 2 * i, p, PIECES)
        return copy(src, dst, KV_FSIB, (j * PIECES + p) * 4 + i, sib)

    def far_z(j, p):
        got(block(bufs[j], 8, p, PIECES), KV_Z, j * PIECES + p)
        far_x(j, p, 0).start()
        far_x(j, p, 1).start()
        far_sib(j, p, 0).start()

    def far_on(p):
        for j in range(2):
            for s in (0, 1):
                got(block(bufs[j], 10 + 2 * s, p, PIECES), KV_FX, (j * PIECES + p) * 2 + s)
            far_two(j, p).start()
            far_sib(j, p, 1).start()
            far_sib(j, p, 2).start()

    def far_last():
        for p in range(PIECES):
            for j in range(2):
                got(block(bufs[j], 14, p, PIECES), KV_FTWO, j * PIECES + p)
                far_sib(j, p, 3).start()

    def far_rest():
        for p in range(PIECES):
            for j in range(2):
                for i in range(4):
                    got(
                        block(bufs[j], 9 + 2 * i, p, PIECES),
                        KV_FSIB, (j * PIECES + p) * 4 + i,
                    )

    def near_on():
        got(block(kbuf, 4), KV_NEAR, 1)
        near_two(0).start()
        got(block(vbuf, 2), KV_NEAR, 2)
        near_two(1).start()
        near_sib(0, 2).start()
        near_sib(1, 1).start()
        got(block(kbuf, 2), KV_NEAR)
        near_sib(0, 1).start()
        got(block(vbuf, 4), KV_NEAR, 3)
        near_sib(1, 2).start()

    def near_last():
        for j in range(2):
            got(block(bufs[j], 6), KV_TWO, j)
            near_sib(j, 3).start()

    def start_near():
        for j in range(2):
            copy(stale[j], block(bufs[j], 2), KV_NEAR, 2 * j, at_x(-1)).start()
            copy(stale[j], block(bufs[j], 4), KV_NEAR, 2 * j + 1, at_x(1)).start()

    for j in range(2):
        copy(stale[j], block(bufs[j], 1), KV_SIB, 4 * j, sib).start()

    @pl.when(is_end)
    def _():
        start_near()
        for j in range(3):
            w_a(j).wait_send()

    @pl.when(is_mid)
    def _():
        for j in range(3):
            got(w_end.at[j, w_rows], W_A, j)
            for d in (1, 2, 3):
                w_b(j, d).start()

    for m in (1, 2):
        @pl.when(t != m)
        def _(m=m):
            o_a(m).wait_send()

    @pl.when(is_mid)
    def _():
        for r in (1, 2, 3):
            got(w_o.at[r, o_rows, o_cols], O_A, r)

    for p in range(PIECES):
        for j in range(2):
            z_piece(j, p).start()

    for c in range(NCH):
        start_img(c)

    def chunk_rows(c, base=0):
        return pl.ds(pl.multiple_of(base + c * CH, CH), CH)

    def norm_chunk(c):
        rows = chunk_rows(c)
        total = jnp.zeros((CH, 1), F32)
        for s in range(4):
            total += jnp.sum(img[s, rows].astype(F32), axis=1, keepdims=True)
        mean = total * (1.0 / DM)
        total = jnp.zeros((CH, 1), F32)
        for s in range(4):
            d = img[s, rows].astype(F32) - mean
            total += jnp.sum(d * d, axis=1, keepdims=True)
        rstd = lax.rsqrt(total * (1.0 / DM) + 1e-06)
        for s in range(4):
            cols = slice(s * SLICE, (s + 1) * SLICE)
            d = (img[s, rows].astype(F32) - mean) * rstd
            modl[rows, cols] = (d * (1.0 + mod[1:2, cols]) + mod[0:1, cols]).astype(BF)

    def project(c, w, put):
        for j in (1, 2, 0):
            y = jnp.dot(modl[chunk_rows(c)], w[j], preferred_element_type=F32)
            if j == 2:
                put(c, j, y.astype(BF))
                continue
            gain = qgain[...] * (LOG2E / math.sqrt(HW)) if j == 0 else kgain[...]
            parts = []
            for h in range(HEADS):
                v = y[:, h * HW : (h + 1) * HW]
                power = jnp.mean(v * v, axis=1, keepdims=True)
                parts.append((v * lax.rsqrt(power + 1e-06) * gain).astype(BF))
            put(c, j, jnp.concatenate(parts, axis=1))

    FRESH = 16 * ROWS

    def qkv_copy(j, c):
        dst = (
            qbuf.at[chunk_rows(c)],
            kbuf.at[chunk_rows(c, FRESH)],
            vbuf.at[chunk_rows(c, FRESH)],
        )[j]
        return copy(stage.at[j, chunk_rows(c)], dst, QKV, j * NCH + c, to_pair)

    def image_chunk(c):
        for r in (1, 2, 3):
            s = lax.rem(t + r, 4)
            got(img.at[s, chunk_rows(c)], IMG, r * NCH + c)
        norm_chunk(c)

    def put_end(c, j, v):
        stage[j, chunk_rows(c)] = v
        qkv_copy(j, c).start()

    def put_own(c, j, v):
        if j == 0:
            qbuf[chunk_rows(c)] = v
        else:
            bufs[j - 1][chunk_rows(c, FRESH)] = v

    def middle_chunk(c):
        @pl.when(c > 0)
        def _():
            image_chunk(c)

        project(c, w_end, put_end)

        @pl.when(c > 0)
        def _():
            project(c, w_own, put_own)

    def end_fresh(c):
        got(kbuf.at[chunk_rows(c, FRESH)], QKV, NCH + c)
        got(vbuf.at[chunk_rows(c, FRESH)], QKV, 2 * NCH + c)

    def end_query(c):
        got(qbuf.at[chunk_rows(c)], QKV, c)

    def fresh_chunk(c):
        @pl.when(is_mid)
        def _():
            middle_chunk(c)

        @pl.when(is_end)
        def _():
            end_fresh(c)
            end_query(c)

    for cp in local:
        cp.wait()

    @pl.when(is_end)
    def _():
        far_z(0, 0)
        far_z(1, 0)
        near_on()
        far_z(0, 1)
        far_z(1, 1)
        far_on(0)
        near_last()
        far_on(1)
        far_last()

    @pl.when(is_mid)
    def _():
        for j in range(3):
            wait_w_b(j)
            for s in (0, 1):
                w_c(j, s).start()
        start_near()
        for d in (1, 2, 3):
            o_b(d).start()
        w_forward(0)
        w_forward(1)
        far_z(0, 0)
        far_z(1, 0)
        w_forward(2)
        near_on()
        w_share(0)
        far_z(0, 1)
        w_share(1)
        far_z(1, 1)
        w_share(2)
        wait_o_b()
        for d in (1, 2, 3):
            o_c(d).start()
        far_on(0)
        near_last()
        image_chunk(0)
        project(0, w_own, put_own)

    def near_rest():
        for j in range(2):
            for i in range(4):
                got(block(bufs[j], 2 * i + 1), KV_SIB, 4 * j + i)

    def attend(c, start, n):
        rows = chunk_rows(c)
        keys = pl.ds(pl.multiple_of(start, ROWS), n)
        for h in range(HEADS):
            cols = slice(h * HW, (h + 1) * HW)
            k = kbuf[keys, cols]
            v = vbuf[keys, cols]
            s = lax.dot_general(
                qbuf[rows, cols], k, (((1,), (1,)), ((), ())), preferred_element_type=F32
            )
            old = m_s[h, rows]
            new = jnp.maximum(old, jnp.max(s, axis=1, keepdims=True))
            shrink = jnp.exp2(old - new)
            p = jnp.exp2(s - new[:, :1]).astype(BF)
            m_s[h, rows] = new
            both = jnp.concatenate([v, jnp.ones_like(v)], axis=1)
            pv = jnp.dot(p, both, preferred_element_type=F32)
            acc_s[h, rows] = acc_s[h, rows] * jnp.concatenate([shrink, shrink], axis=1) + pv

    other = jnp.where(is_mid, 3 - t, pair)
    from_end = lax.rem(pair - t + 4, 4)

    def tail_copy(c):
        rows = chunk_rows(c)
        r = lax.rem(t - other + 4, 4)
        return copy(att.at[0, rows], att.at[r, rows], TAIL, r * NCH + c, {"tensor": other})

    def relay_copy(c):
        rows = chunk_rows(c)
        src = att.at[from_end, rows]
        return copy(src, att.at[2, rows], TAIL, 2 * NCH + c, {"tensor": other})

    def relay(c):
        got(att.at[from_end, chunk_rows(c)], TAIL, from_end * NCH + c)
        relay_copy(c).start()

    def finish(c):
        attend(c, FRESH, ROWS)
        rows = chunk_rows(c)
        for h in range(HEADS):
            a = acc_s[h, rows]
            att[0, rows, h * HW : (h + 1) * HW] = (a[:, :HW] / a[:, HW:]).astype(BF)
        tail_copy(c).start()

    def out_copy(c):
        return copy(ostage.at[chunk_rows(c)], out.at[chunk_rows(c)], OUT, c, to_pair)

    def project_out(c):
        rows = chunk_rows(c)
        r = 4 - from_end
        got(att.at[r, rows], TAIL, r * NCH + c)
        got(att.at[2, rows], TAIL, 2 * NCH + c)
        for half, cols in ((1, pair_cols), (0, my_cols)):
            y = jnp.zeros((CH, SLICE), F32)
            for r in range(4):
                w = w_o[r, :, half * SLICE : (half + 1) * SLICE]
                y += jnp.dot(att[r, rows], w, preferred_element_type=F32)
            y = (y * mod[2:3, cols]).astype(BF)
            if half:
                ostage[rows] = y
                out_copy(c).start()
            else:
                out[rows] = y

    @pl.when(is_mid)
    def _():
        for cp in local_o:
            cp.wait()
        for j in range(3):
            rows = pl.ds(pl.multiple_of((1 - cc) * 1536, 1536), 1536)
            got(w_end.at[j, rows], W_D, j)

    def near(c):
        @pl.loop(0, 4096 // KB)
        def _(b):
            attend(c, b * KB, KB)

    def distant(c):
        @pl.loop(4096 // KB, 8192 // KB)
        def _(b):
            attend(c, b * KB, KB)

    @pl.loop(0, NCH - 1)
    def _(c):
        fresh_chunk(c)

        @pl.when(c == 0)
        def _():
            near_rest()

        near(c)

        @pl.when((c == 1) & is_mid)
        def _():
            far_on(1)

        @pl.when((c == 2) & is_mid)
        def _():
            far_last()

        @pl.when((c == 1) & is_end)
        def _():
            far_rest()

        @pl.when((c > 0) & is_end)
        def _():
            distant(c - 1)

    @pl.when(is_mid)
    def _():
        middle_chunk(NCH - 1)
        wait_o_c()
        o_d().start()
        far_rest()

        @pl.loop(0, NCH - 1)
        def _(c):
            distant(c)
            finish(c)

    @pl.when(is_end)
    def _():
        distant(NCH - 2)
        end_fresh(NCH - 1)

        @pl.loop(0, NCH - 1)
        def _(c):
            finish(c)

        end_query(NCH - 1)

    @pl.loop(0, 8192 // KB)
    def _(b):
        attend(NCH - 1, b * KB, KB)

        @pl.when((b > 0) & is_mid)
        def _():
            relay(b - 1)

            @pl.when(b == 8192 // KB - 1)
            def _():
                got(w_o.at[pl.ds(1, 3), pl.ds(pl.multiple_of((1 - cc) * 192, 192), 192)], O_D)
                project_out(0)

    finish(NCH - 1)

    @pl.when(is_mid)
    def _():
        @pl.loop(1, NCH)
        def _(c):
            @pl.when(c == 2)
            def _():
                relay(NCH - 1)

            project_out(c)

    @pl.when(is_end)
    def _():
        for c in range(NCH):
            got(out.at[chunk_rows(c)], OUT, c)

    for j in range(2):
        for p in range(PIECES):
            z_piece(j, p).wait_send()
            far_two(j, p).wait_send()
            for s in range(2):
                far_x(j, p, s).wait_send()
            for i in range(4):
                far_sib(j, p, i).wait_send()
        for s in range(2):
            copy(stale[j], block(bufs[j], 2), KV_NEAR, 2 * j + s, at_x(1)).wait_send()
        for i in range(4):
            near_sib(j, i).wait_send()
        near_two(j).wait_send()

    for m in (1, 2):
        @pl.when(t != m)
        def _(m=m):
            for c in range(NCH):
                img_copy(m, c).wait_send()

    for c in range(NCH):
        tail_copy(c).wait_send()

    @pl.when(is_mid)
    def _():
        for d in (1, 2, 3):
            for j in range(3):
                w_b(j, d).wait_send()
            o_b(d).wait_send()
            o_c(d).wait_send()
        for j in range(3):
            w_d(j).wait_send()
            for s in (0, 1):
                w_c(j, s).wait_send()
                w_two(j, s).wait_send()
        o_d().wait_send()
        for c in range(NCH):
            out_copy(c).wait_send()
            relay_copy(c).wait_send()
            for j in range(3):
                qkv_copy(j, c).wait_send()


def shards(image, modulation, w_query, w_key, w_value, w_out, query_gain, key_gain, text_keys, text_values, stale_keys, stale_values):
    hbm = pl.BlockSpec(memory_space=pl.ANY)
    vmem = pl.BlockSpec(memory_space=pltpu.VMEM)
    return pl.pallas_call(
        kernel,
        out_shape=jax.ShapeDtypeStruct((ROWS, SLICE), BF),
        in_specs=[hbm, vmem, hbm, hbm, hbm, hbm, vmem, vmem, hbm, hbm, hbm, hbm],
        out_specs=vmem,
        scratch_shapes=[
            pltpu.VMEM((17 * ROWS, WIDE), BF),
            pltpu.VMEM((17 * ROWS, WIDE), BF),
            pltpu.VMEM((4, ROWS, SLICE), BF),
            pltpu.VMEM((3, DM, WIDE), BF),
            pltpu.VMEM((3, DM, WIDE), BF),
            pltpu.VMEM((4, WIDE, 2 * SLICE), BF),
            pltpu.VMEM((ROWS, DM), BF),
            pltpu.VMEM((ROWS, WIDE), BF),
            pltpu.VMEM((3, ROWS, WIDE), BF),
            pltpu.VMEM((4, ROWS, WIDE), BF),
            pltpu.VMEM((ROWS, SLICE), BF),
            pltpu.VMEM((HEADS, ROWS, HW), F32),
            pltpu.VMEM((HEADS, ROWS, 2 * HW), F32),
            pltpu.SemaphoreType.DMA((NSEM,)),
            pltpu.SemaphoreType.DMA((NSEM,)),
            pltpu.SemaphoreType.DMA((8,)),
        ],
        compiler_params=pltpu.CompilerParams(
            collective_id=0, has_side_effects=True, vmem_limit_bytes=60 * 1024 * 1024
        ),
        cost_estimate=pl.CostEstimate(
            flops=12_000_000_000, bytes_accessed=20_000_000, transcendentals=14_000_000
        ),
        name="joint_attention",
    )(
        image, modulation, w_query, w_key, w_value, w_out,
        query_gain.reshape(1, HW), key_gain.reshape(1, HW),
        text_keys, text_values, stale_keys, stale_values,
    )


def solution(mesh):
    rows = P(("batch", "patch"), "tensor")
    cols = P(None, "tensor")
    in_specs = (
        rows, P("batch", None), cols, cols, cols, P("tensor", None), P(), P(),
        P("batch", "tensor"), P("batch", "tensor"), rows, rows,
    )
    return jax.shard_map(shards, mesh=mesh, in_specs=in_specs, out_specs=rows, check_vma=False)
```

```python
import functools
import math

import jax
import jax.numpy as jnp
from jax import lax
from jax.experimental import pallas as pl
from jax.experimental.pallas import tpu as pltpu
from jax.sharding import PartitionSpec as P

MESH = pl.DeviceIdType.MESH
BF = jnp.bfloat16
F32 = jnp.float32
ROWS = 512
HW = 128
HEADS = 3
WIDE = HEADS * HW
SLICE = 768
DM = 4 * SLICE
CH = 128
NCH = ROWS // CH
KB = 2048
PIECES = 2
LOG2E = 1.4426950408889634

KV_NEAR = 0
KV_TWO = KV_NEAR + 4
KV_SIB = KV_TWO + 2
KV_Z = KV_SIB + 8
KV_FX = KV_Z + 2 * PIECES
KV_FTWO = KV_FX + 4 * PIECES
KV_FSIB = KV_FTWO + 2 * PIECES
W_A = KV_FSIB + 8 * PIECES
W_B = W_A + 3
W_C = W_B + 9
W_D = W_C + 12
O_A = W_D + 3
O_B = O_A + 4
O_C = O_B + 3
O_D = O_C + 3
IMG = O_D + 1
QKV = IMG + 4 * NCH
TAIL = QKV + 3 * NCH
OUT = TAIL + 4 * NCH
NSEM = OUT + NCH


def kernel(
    img_h, mod, wq_h, wk_h, wv_h, wo_h, qgain, kgain, tk_h, tv_h, sk_h, sv_h,
    out,
    kbuf, vbuf, img, w_own, w_end, w_o, modl, qbuf, stage, att, ostage, m_s, acc_s,
    ssem, rsem, lsem,
):
    yy = lax.axis_index("batch")
    patch = lax.axis_index("patch")
    t = lax.axis_index("tensor")
    zh = patch // 8
    xx = lax.rem(patch, 8) // 2
    cc = lax.rem(patch, 2)
    is_mid = (t == 1) | (t == 2)
    is_end = (t == 0) | (t == 3)
    pair = jnp.where(t < 2, 1 - t, 5 - t)

    def at_x(d):
        return {"patch": zh * 8 + lax.rem(xx + d + 4, 4) * 2 + cc}

    def at_y(d):
        return {"batch": lax.rem(yy + d + 4, 4)}

    sib = {"patch": zh * 8 + xx * 2 + (1 - cc)}
    far = {"patch": (1 - zh) * 8 + xx * 2 + cc}
    to_pair = {"tensor": pair}

    def copy(src, dst, base, off, dev):
        i = base + off
        return pltpu.make_async_remote_copy(
            src_ref=src, dst_ref=dst, send_sem=ssem.at[i], recv_sem=rsem.at[i],
            device_id=dev, device_id_type=MESH,
        )

    def got(dst, base, off=0):
        copy(dst, dst, base, off, sib).wait_recv()

    def block(buf, slot, piece=0, pieces=1):
        n = ROWS // pieces
        return buf.at[pl.ds(slot * ROWS + piece * n, n)]

    local = [
        pltpu.make_async_copy(wq_h, w_own.at[0], lsem.at[0]),
        pltpu.make_async_copy(wk_h, w_own.at[1], lsem.at[1]),
        pltpu.make_async_copy(wv_h, w_own.at[2], lsem.at[2]),
        pltpu.make_async_copy(tk_h, block(kbuf, 0), lsem.at[3]),
        pltpu.make_async_copy(tv_h, block(vbuf, 0), lsem.at[4]),
        pltpu.make_async_copy(img_h, img.at[t], lsem.at[5]),
    ]
    my_cols = pl.ds(pl.multiple_of(t * SLICE, SLICE), SLICE)
    pair_cols = pl.ds(pl.multiple_of(pair * SLICE, SLICE), SLICE)
    local_o = [
        pltpu.make_async_copy(wo_h.at[:, my_cols], w_o.at[0, :, pl.ds(0, SLICE)], lsem.at[6]),
        pltpu.make_async_copy(wo_h.at[:, pair_cols], w_o.at[0, :, pl.ds(SLICE, SLICE)], lsem.at[7]),
    ]

    for cp in local:
        cp.start()

    @pl.when(is_mid)
    def _():
        for cp in local_o:
            cp.start()

    peers = [sib, far] + [at_x(d) for d in (1, 2, 3)] + [at_y(d) for d in (1, 2, 3)]
    peers += [{"tensor": lax.rem(t + d, 4)} for d in (1, 2, 3)]
    barrier = pltpu.get_barrier_semaphore()
    for p in peers:
        pl.semaphore_signal(barrier, inc=1, device_id=p, device_id_type=MESH)
    pl.semaphore_wait(barrier, len(peers))

    stale = (sk_h, sv_h)
    bufs = (kbuf, vbuf)

    def z_piece(j, p):
        n = ROWS // PIECES
        return copy(
            stale[j].at[pl.ds(p * n, n)], block(bufs[j], 8, p, PIECES), KV_Z, j * PIECES + p, far
        )

    w_rows = pl.ds(pl.multiple_of(cc * 1536 + yy * 384 + xx * 96, 96), 96)

    def w_a(j):
        return copy((wq_h, wk_h, wv_h)[j].at[w_rows], w_end.at[j, w_rows], W_A, j, to_pair)

    @pl.when(is_end)
    def _():
        for j in range(3):
            w_a(j).start()

    def img_copy(m, c):
        r = lax.rem(t - m + 4, 4)
        rows = pl.ds(pl.multiple_of(c * CH, CH), CH)
        return copy(img_h.at[rows], img.at[t, rows], IMG, r * NCH + c, {"tensor": jnp.int32(m)})

    def start_img(c):
        for m in (1, 2):
            @pl.when(t != m)
            def _(m=m):
                img_copy(m, c).start()

    o_rows = pl.ds(pl.multiple_of(cc * 192 + yy * 48, 48), 48)
    o_cols = pl.ds(pl.multiple_of(xx * 384, 384), 384)

    def o_a(m):
        r = lax.rem(t - m + 4, 4)
        e = 3 * (m - 1)
        start = jnp.where(xx < 2, m, e) * SLICE + lax.rem(xx, 2) * 384
        src = wo_h.at[o_rows, pl.ds(pl.multiple_of(start, 384), 384)]
        return copy(src, w_o.at[r, o_rows, o_cols], O_A, r, {"tensor": jnp.int32(m)})

    for m in (1, 2):
        @pl.when(t != m)
        def _(m=m):
            o_a(m).start()

    m_s[...] = jnp.full(m_s.shape, -1e30, F32)
    acc_s[...] = jnp.zeros(acc_s.shape, F32)

    def w_b(j, d):
        piece = w_end.at[j, w_rows]
        return copy(piece, piece, W_B, 3 * j + d - 1, at_x(d))

    def y_rows(d, half=None):
        n = 384 if half is None else 192
        first = cc * 1536 + lax.rem(yy + d + 4, 4) * 384 + (192 if half else 0)
        return pl.ds(pl.multiple_of(first, n), n)

    def w_c(j, s):
        piece = w_end.at[j, y_rows(0)]
        return copy(piece, piece, W_C, 2 * j + s, at_y(1 - 2 * s))

    def w_two(j, s):
        piece = w_end.at[j, y_rows(2 * s - 1, s)]
        return copy(piece, piece, W_C, 6 + 2 * j + s, at_y(1 - 2 * s))

    def w_d(j):
        piece = w_end.at[j, pl.ds(pl.multiple_of(cc * 1536, 1536), 1536)]
        return copy(piece, piece, W_D, j, sib)

    def w_forward(j):
        for s in (0, 1):
            got(w_end.at[j, y_rows(2 * s - 1)], W_C, 2 * j + s)
            w_two(j, s).start()

    def w_share(j):
        for s in (0, 1):
            got(w_end.at[j, y_rows(2, s)], W_C, 6 + 2 * j + s)
        w_d(j).start()

    def o_b(d):
        piece = w_o.at[pl.ds(1, 3), o_rows, o_cols]
        return copy(piece, piece, O_B, d - 1, at_x(d))

    def o_c(d):
        piece = w_o.at[pl.ds(1, 3), o_rows]
        return copy(piece, piece, O_C, d - 1, at_y(d))

    def o_d():
        piece = w_o.at[pl.ds(1, 3), pl.ds(pl.multiple_of(cc * 192, 192), 192)]
        return copy(piece, piece, O_D, 0, sib)

    def wait_w_b(j):
        for d in (1, 2, 3):
            rows = pl.ds(pl.multiple_of(cc * 1536 + yy * 384 + lax.rem(xx - d + 4, 4) * 96, 96), 96)
            got(w_end.at[j, rows], W_B, 3 * j + d - 1)

    def wait_o_b():
        for d in (1, 2, 3):
            cols = pl.ds(pl.multiple_of(lax.rem(xx - d + 4, 4) * 384, 384), 384)
            got(w_o.at[pl.ds(1, 3), o_rows, cols], O_B, d - 1)

    def wait_o_c():
        for d in (1, 2, 3):
            rows = pl.ds(pl.multiple_of(cc * 192 + lax.rem(yy - d + 4, 4) * 48, 48), 48)
            got(w_o.at[pl.ds(1, 3), rows], O_C, d - 1)

    def near_sib(j, i):
        src = stale[j] if i == 0 else block(bufs[j], 2 * i)
        return copy(src, block(bufs[j], 2 * i + 1), KV_SIB, 4 * j + i, sib)

    def near_two(j):
        if j == 0:
            return copy(block(kbuf, 4), block(kbuf, 6), KV_TWO, 0, at_x(1))
        return copy(block(vbuf, 2), block(vbuf, 6), KV_TWO, 1, at_x(-1))

    def far_x(j, p, s):
        src = block(bufs[j], 8, p, PIECES)
        dst = block(bufs[j], 10 + 2 * s, p, PIECES)
        return copy(src, dst, KV_FX, (j * PIECES + p) * 2 + s, at_x(-1 if s == 0 else 1))

    def far_two(j, p):
        src = block(bufs[j], 12 if j == 0 else 10, p, PIECES)
        dst = block(bufs[j], 14, p, PIECES)
        return copy(src, dst, KV_FTWO, j * PIECES + p, at_x(1 if j == 0 else -1))

    def far_sib(j, p, i):
        src = block(bufs[j], 8 + 2 * i, p, PIECES)
        dst = block(bufs[j], 9 + 2 * i, p, PIECES)
        return copy(src, dst, KV_FSIB, (j * PIECES + p) * 4 + i, sib)

    def far_z(j, p):
        got(block(bufs[j], 8, p, PIECES), KV_Z, j * PIECES + p)
        far_x(j, p, 0).start()
        far_x(j, p, 1).start()
        far_sib(j, p, 0).start()

    def far_on(p):
        for j in range(2):
            for s in (0, 1):
                got(block(bufs[j], 10 + 2 * s, p, PIECES), KV_FX, (j * PIECES + p) * 2 + s)
            far_two(j, p).start()
            far_sib(j, p, 1).start()
            far_sib(j, p, 2).start()

    def far_last():
        for p in range(PIECES):
            for j in range(2):
                got(block(bufs[j], 14, p, PIECES), KV_FTWO, j * PIECES + p)
                far_sib(j, p, 3).start()

    def far_rest():
        for p in range(PIECES):
            for j in range(2):
                for i in range(4):
                    got(
                        block(bufs[j], 9 + 2 * i, p, PIECES),
                        KV_FSIB, (j * PIECES + p) * 4 + i,
                    )

    def near_on():
        got(block(kbuf, 4), KV_NEAR, 1)
        near_two(0).start()
        got(block(vbuf, 2), KV_NEAR, 2)
        near_two(1).start()
        near_sib(0, 2).start()
        near_sib(1, 1).start()
        got(block(kbuf, 2), KV_NEAR)
        near_sib(0, 1).start()
        got(block(vbuf, 4), KV_NEAR, 3)
        near_sib(1, 2).start()

    def near_last():
        for j in range(2):
            got(block(bufs[j], 6), KV_TWO, j)
            near_sib(j, 3).start()

    def start_near():
        for j in range(2):
            copy(stale[j], block(bufs[j], 2), KV_NEAR, 2 * j, at_x(-1)).start()
            copy(stale[j], block(bufs[j], 4), KV_NEAR, 2 * j + 1, at_x(1)).start()

    for j in range(2):
        copy(stale[j], block(bufs[j], 1), KV_SIB, 4 * j, sib).start()

    @pl.when(is_end)
    def _():
        start_near()
        for j in range(3):
            w_a(j).wait_send()

    @pl.when(is_mid)
    def _():
        for j in range(3):
            got(w_end.at[j, w_rows], W_A, j)
            for d in (1, 2, 3):
                w_b(j, d).start()
        start_near()

    for m in (1, 2):
        @pl.when(t != m)
        def _(m=m):
            o_a(m).wait_send()

    @pl.when(is_mid)
    def _():
        for r in (1, 2, 3):
            got(w_o.at[r, o_rows, o_cols], O_A, r)

    for p in range(PIECES):
        for j in range(2):
            z_piece(j, p).start()

    for c in range(NCH):
        start_img(c)

    def chunk_rows(c, base=0):
        return pl.ds(pl.multiple_of(base + c * CH, CH), CH)

    def norm_chunk(c):
        rows = chunk_rows(c)
        total = jnp.zeros((CH, 1), F32)
        for s in range(4):
            total += jnp.sum(img[s, rows].astype(F32), axis=1, keepdims=True)
        mean = total * (1.0 / DM)
        total = jnp.zeros((CH, 1), F32)
        for s in range(4):
            d = img[s, rows].astype(F32) - mean
            total += jnp.sum(d * d, axis=1, keepdims=True)
        rstd = lax.rsqrt(total * (1.0 / DM) + 1e-06)
        for s in range(4):
            cols = slice(s * SLICE, (s + 1) * SLICE)
            d = (img[s, rows].astype(F32) - mean) * rstd
            modl[rows, cols] = (d * (1.0 + mod[1:2, cols]) + mod[0:1, cols]).astype(BF)

    def project(c, w, put):
        for j in (1, 2, 0):
            y = jnp.dot(modl[chunk_rows(c)], w[j], preferred_element_type=F32)
            if j == 2:
                put(c, j, y.astype(BF))
                continue
            gain = qgain[...] * (LOG2E / math.sqrt(HW)) if j == 0 else kgain[...]
            parts = []
            for h in range(HEADS):
                v = y[:, h * HW : (h + 1) * HW]
                power = jnp.mean(v * v, axis=1, keepdims=True)
                parts.append((v * lax.rsqrt(power + 1e-06) * gain).astype(BF))
            put(c, j, jnp.concatenate(parts, axis=1))

    FRESH = 16 * ROWS

    def qkv_copy(j, c):
        dst = (
            qbuf.at[chunk_rows(c)],
            kbuf.at[chunk_rows(c, FRESH)],
            vbuf.at[chunk_rows(c, FRESH)],
        )[j]
        return copy(stage.at[j, chunk_rows(c)], dst, QKV, j * NCH + c, to_pair)

    def image_chunk(c):
        for r in (1, 2, 3):
            s = lax.rem(t + r, 4)
            got(img.at[s, chunk_rows(c)], IMG, r * NCH + c)
        norm_chunk(c)

    def put_end(c, j, v):
        stage[j, chunk_rows(c)] = v
        qkv_copy(j, c).start()

    def put_own(c, j, v):
        if j == 0:
            qbuf[chunk_rows(c)] = v
        else:
            bufs[j - 1][chunk_rows(c, FRESH)] = v

    def middle_chunk(c):
        @pl.when(c > 0)
        def _():
            image_chunk(c)

        project(c, w_end, put_end)

        @pl.when(c > 0)
        def _():
            project(c, w_own, put_own)

    def end_fresh(c):
        got(kbuf.at[chunk_rows(c, FRESH)], QKV, NCH + c)
        got(vbuf.at[chunk_rows(c, FRESH)], QKV, 2 * NCH + c)

    def end_query(c):
        got(qbuf.at[chunk_rows(c)], QKV, c)

    def fresh_chunk(c):
        @pl.when(is_mid)
        def _():
            middle_chunk(c)

        @pl.when(is_end)
        def _():
            end_fresh(c)
            end_query(c)

    for cp in local:
        cp.wait()

    @pl.when(is_end)
    def _():
        far_z(0, 0)
        far_z(1, 0)
        near_on()
        far_z(0, 1)
        far_z(1, 1)
        far_on(0)
        near_last()
        far_on(1)
        far_last()

    @pl.when(is_mid)
    def _():
        for j in range(3):
            wait_w_b(j)
            for s in (0, 1):
                w_c(j, s).start()
        w_forward(0)
        w_forward(1)
        far_z(0, 0)
        far_z(1, 0)
        w_forward(2)
        near_on()
        w_share(0)
        far_z(0, 1)
        w_share(1)
        far_z(1, 1)
        w_share(2)
        far_on(0)
        near_last()
        for d in (1, 2, 3):
            o_b(d).start()
        image_chunk(0)
        project(0, w_own, put_own)

    def near_rest():
        for j in range(2):
            for i in range(4):
                got(block(bufs[j], 2 * i + 1), KV_SIB, 4 * j + i)

    def attend(c, start, n):
        rows = chunk_rows(c)
        keys = pl.ds(pl.multiple_of(start, ROWS), n)
        for h in range(HEADS):
            cols = slice(h * HW, (h + 1) * HW)
            k = kbuf[keys, cols]
            v = vbuf[keys, cols]
            s = lax.dot_general(
                qbuf[rows, cols], k, (((1,), (1,)), ((), ())), preferred_element_type=F32
            )
            old = m_s[h, rows]
            new = jnp.maximum(old, jnp.max(s, axis=1, keepdims=True))
            shrink = jnp.exp2(old - new)
            p = jnp.exp2(s - new[:, :1]).astype(BF)
            m_s[h, rows] = new
            both = jnp.concatenate([v, jnp.ones_like(v)], axis=1)
            pv = jnp.dot(p, both, preferred_element_type=F32)
            acc_s[h, rows] = acc_s[h, rows] * jnp.concatenate([shrink, shrink], axis=1) + pv

    other = jnp.where(is_mid, 3 - t, pair)
    from_end = lax.rem(pair - t + 4, 4)

    def tail_copy(c):
        rows = chunk_rows(c)
        r = lax.rem(t - other + 4, 4)
        return copy(att.at[0, rows], att.at[r, rows], TAIL, r * NCH + c, {"tensor": other})

    def relay_copy(c):
        rows = chunk_rows(c)
        src = att.at[from_end, rows]
        return copy(src, att.at[2, rows], TAIL, 2 * NCH + c, {"tensor": other})

    def relay(c):
        got(att.at[from_end, chunk_rows(c)], TAIL, from_end * NCH + c)
        relay_copy(c).start()

    def finish(c):
        attend(c, FRESH, ROWS)
        rows = chunk_rows(c)
        for h in range(HEADS):
            a = acc_s[h, rows]
            att[0, rows, h * HW : (h + 1) * HW] = (a[:, :HW] / a[:, HW:]).astype(BF)
        tail_copy(c).start()

    def out_copy(c):
        return copy(ostage.at[chunk_rows(c)], out.at[chunk_rows(c)], OUT, c, to_pair)

    def project_out(c):
        rows = chunk_rows(c)
        r = 4 - from_end
        got(att.at[r, rows], TAIL, r * NCH + c)
        got(att.at[2, rows], TAIL, 2 * NCH + c)
        for half, cols in ((1, pair_cols), (0, my_cols)):
            y = jnp.zeros((CH, SLICE), F32)
            for r in range(4):
                w = w_o[r, :, half * SLICE : (half + 1) * SLICE]
                y += jnp.dot(att[r, rows], w, preferred_element_type=F32)
            y = (y * mod[2:3, cols]).astype(BF)
            if half:
                ostage[rows] = y
                out_copy(c).start()
            else:
                out[rows] = y

    @pl.when(is_mid)
    def _():
        for cp in local_o:
            cp.wait()
        for j in range(3):
            rows = pl.ds(pl.multiple_of((1 - cc) * 1536, 1536), 1536)
            got(w_end.at[j, rows], W_D, j)

    def near(c):
        @pl.loop(0, 4096 // KB)
        def _(b):
            attend(c, b * KB, KB)

    def distant(c):
        @pl.loop(4096 // KB, 8192 // KB)
        def _(b):
            attend(c, b * KB, KB)

    @pl.loop(0, NCH - 1)
    def _(c):
        fresh_chunk(c)

        @pl.when(c == 0)
        def _():
            near_rest()

        near(c)

        @pl.when((c == 1) & is_mid)
        def _():
            far_on(1)
            wait_o_b()
            for d in (1, 2, 3):
                o_c(d).start()

        @pl.when((c == 2) & is_mid)
        def _():
            far_last()

        @pl.when((c == 1) & is_end)
        def _():
            far_rest()

        @pl.when((c > 0) & is_end)
        def _():
            distant(c - 1)

    @pl.when(is_mid)
    def _():
        middle_chunk(NCH - 1)
        far_rest()

        @pl.loop(0, NCH - 1)
        def _(c):
            distant(c)
            finish(c)

        wait_o_c()
        o_d().start()

    @pl.when(is_end)
    def _():
        distant(NCH - 2)
        end_fresh(NCH - 1)

        @pl.loop(0, NCH - 1)
        def _(c):
            finish(c)

        end_query(NCH - 1)

    @pl.loop(0, 8192 // KB)
    def _(b):
        attend(NCH - 1, b * KB, KB)

        @pl.when((b > 0) & is_mid)
        def _():
            relay(b - 1)

            @pl.when(b == 2)
            def _():
                got(w_o.at[pl.ds(1, 3), pl.ds(pl.multiple_of((1 - cc) * 192, 192), 192)], O_D)

            @pl.when(b > 1)
            def _():
                project_out(b - 2)

    finish(NCH - 1)

    @pl.when(is_mid)
    def _():
        @pl.loop(2, NCH)
        def _(c):
            @pl.when(c == 2)
            def _():
                relay(NCH - 1)

            project_out(c)

    @pl.when(is_end)
    def _():
        for c in range(NCH):
            got(out.at[chunk_rows(c)], OUT, c)

    for j in range(2):
        for p in range(PIECES):
            z_piece(j, p).wait_send()
            far_two(j, p).wait_send()
            for s in range(2):
                far_x(j, p, s).wait_send()
            for i in range(4):
                far_sib(j, p, i).wait_send()
        for s in range(2):
            copy(stale[j], block(bufs[j], 2), KV_NEAR, 2 * j + s, at_x(1)).wait_send()
        for i in range(4):
            near_sib(j, i).wait_send()
        near_two(j).wait_send()

    for m in (1, 2):
        @pl.when(t != m)
        def _(m=m):
            for c in range(NCH):
                img_copy(m, c).wait_send()

    for c in range(NCH):
        tail_copy(c).wait_send()

    @pl.when(is_mid)
    def _():
        for d in (1, 2, 3):
            for j in range(3):
                w_b(j, d).wait_send()
            o_b(d).wait_send()
            o_c(d).wait_send()
        for j in range(3):
            w_d(j).wait_send()
            for s in (0, 1):
                w_c(j, s).wait_send()
                w_two(j, s).wait_send()
        o_d().wait_send()
        for c in range(NCH):
            out_copy(c).wait_send()
            relay_copy(c).wait_send()
            for j in range(3):
                qkv_copy(j, c).wait_send()


def shards(image, modulation, w_query, w_key, w_value, w_out, query_gain, key_gain, text_keys, text_values, stale_keys, stale_values):
    hbm = pl.BlockSpec(memory_space=pl.ANY)
    vmem = pl.BlockSpec(memory_space=pltpu.VMEM)
    return pl.pallas_call(
        kernel,
        out_shape=jax.ShapeDtypeStruct((ROWS, SLICE), BF),
        in_specs=[hbm, vmem, hbm, hbm, hbm, hbm, vmem, vmem, hbm, hbm, hbm, hbm],
        out_specs=vmem,
        scratch_shapes=[
            pltpu.VMEM((17 * ROWS, WIDE), BF),
            pltpu.VMEM((17 * ROWS, WIDE), BF),
            pltpu.VMEM((4, ROWS, SLICE), BF),
            pltpu.VMEM((3, DM, WIDE), BF),
            pltpu.VMEM((3, DM, WIDE), BF),
            pltpu.VMEM((4, WIDE, 2 * SLICE), BF),
            pltpu.VMEM((ROWS, DM), BF),
            pltpu.VMEM((ROWS, WIDE), BF),
            pltpu.VMEM((3, ROWS, WIDE), BF),
            pltpu.VMEM((4, ROWS, WIDE), BF),
            pltpu.VMEM((ROWS, SLICE), BF),
            pltpu.VMEM((HEADS, ROWS, HW), F32),
            pltpu.VMEM((HEADS, ROWS, 2 * HW), F32),
            pltpu.SemaphoreType.DMA((NSEM,)),
            pltpu.SemaphoreType.DMA((NSEM,)),
            pltpu.SemaphoreType.DMA((8,)),
        ],
        compiler_params=pltpu.CompilerParams(
            collective_id=0, has_side_effects=True, vmem_limit_bytes=60 * 1024 * 1024
        ),
        cost_estimate=pl.CostEstimate(
            flops=12_000_000_000, bytes_accessed=20_000_000, transcendentals=14_000_000
        ),
        name="joint_attention",
    )(
        image, modulation, w_query, w_key, w_value, w_out,
        query_gain.reshape(1, HW), key_gain.reshape(1, HW),
        text_keys, text_values, stale_keys, stale_values,
    )


def solution(mesh):
    rows = P(("batch", "patch"), "tensor")
    cols = P(None, "tensor")
    in_specs = (
        rows, P("batch", None), cols, cols, cols, P("tensor", None), P(), P(),
        P("batch", "tensor"), P("batch", "tensor"), rows, rows,
    )
    return jax.shard_map(shards, mesh=mesh, in_specs=in_specs, out_specs=rows, check_vma=False)
```
